128 devices in a mesh: space: 32 (over z_lo, x, y), chan: 4 (over z_hi, core).
Axes of the slice: x: 4, y: 4, z: 4 (z_hi: 2, z_lo: 2; z = z_hi * 2 + z_lo), core: 2. Of those that a mesh axis runs over, the one named last changes fastest.
Arguments:
- volume: bfloat16 [4, 512, 32, 512], P(None, 'space', 'chan'), may hold values from -6 to 6
- kernel_one: bfloat16 [3, 3, 3, 4, 32], replicated, may hold values from -0.625 to 0.625
- kernel_two: bfloat16 [3, 3, 3, 32, 64], replicated, may hold values from -0.21875 to 0.21875
- kernel_three: bfloat16 [3, 3, 3, 64, 128], P(None, None, None, 'chan'), may hold values from -0.15625 to 0.15625
- kernel_four: bfloat16 [3, 3, 3, 128, 256], P(None, None, None, 'chan'), may hold values from -0.109375 to 0.109375
- cotangent: bfloat16 [256, 128, 8, 128], P('chan', 'space'), may hold values from -0.15625 to 0.15625
Outputs:
- features: bfloat16 [256, 128, 8, 128], P('chan', 'space')
- grad_one: float32 [3, 3, 3, 4, 32], replicated
- grad_two: float32 [3, 3, 3, 32, 64], replicated
- grad_three: float32 [3, 3, 3, 64, 128], P(None, None, None, 'chan')
- grad_four: float32 [3, 3, 3, 128, 256], P(None, None, None, 'chan')
The draws below stay inside these ranges and needn't reach their ends.
All inputs are finite; a program needn't handle non-finite values.
Results may differ from the reference program's by a relative error of at most 0.014.
Values may be sent and summed in bfloat16 or wider, within the bound.
No kernel may reach another device: no remote copies, remote signals or barrier semaphores. Data moves between devices by JAX's collectives and lax.ppermute only.
A program may use at most 192 MiB of HBM per device.

```python
import jax
import jax.numpy as jnp
from jax import lax

C0 = 4
C1 = 32
C2 = 64
C3 = 128
C4 = 256
WID = 512
DEPTH = 512
HEIGHT = 32


def steps_of(own_key, extent, shards, smallest, top_value):
    factor_of, own = 1.0, jax.random.fold_in(own_key, 6)
    for position, blocks in shards:
        heights = jnp.exp(jax.random.uniform(jax.random.fold_in(own, position), (blocks,), jnp.float32, smallest / len(shards), top_value / len(shards)))
        factor_of = factor_of * jnp.repeat(heights, extent[position] // blocks).reshape([-1 if axis == position else 1 for axis in range(len(extent))])
    return factor_of


def normal_values(rng, extent, width, bound, split=(), kind=jnp.bfloat16):
    gain = steps_of(rng, extent, split, -0.22, 0.18) if split else 1.0
    entries = jax.random.normal(rng, extent, jnp.float32) * width * gain
    return jnp.minimum(jnp.maximum(entries, -bound), bound).astype(kind)


def setup_inputs(seed: int = 0) -> dict:
    key_list = jax.random.split(jax.random.key(seed), 7)
    volume = normal_values(key_list[0], (C0, DEPTH, HEIGHT, WID), 1.0, 6.0, ((1, 32), (2, 4)))
    kernel_one = normal_values(key_list[1], (3, 3, 3, C0, C1), (27 * C0) ** -0.5, 0.625)
    kernel_two = normal_values(key_list[2], (3, 3, 3, C1, C2), (27 * C1) ** -0.5, 0.21875)
    kernel_three = normal_values(key_list[3], (3, 3, 3, C2, C3), (27 * C2) ** -0.5, 0.15625, ((3, 4),))
    kernel_four = normal_values(key_list[4], (3, 3, 3, C3, C4), (27 * C3) ** -0.5, 0.109375, ((3, 4),))
    cotangent = normal_values(key_list[5], (C4, DEPTH // 4, HEIGHT // 4, WID // 4), (4.0 / (DEPTH * HEIGHT * WID // 64) ** 0.5), 0.15625, ((0, 4), (1, 32)))
    return {"volume": volume, "kernel_one": kernel_one, "kernel_two": kernel_two, "kernel_three": kernel_three, "kernel_four": kernel_four, "cotangent": cotangent}


NUMBERS = ('NCDHW', 'DHWIO', 'NCDHW')

def convolve(field, kernel, stride, pads):
    result = lax.conv_general_dilated(field[None].astype(jnp.float32), kernel.astype(jnp.float32), (stride, stride, stride), [pads, pads, pads], dimension_numbers=NUMBERS, precision=lax.Precision.HIGHEST, preferred_element_type=jnp.float32)
    return result[0]

def silu_slope(value):
    sigma = jax.nn.sigmoid(value)
    return sigma * (1.0 + value * (1.0 - sigma))

def layer(field, kernel, stride, pads):

    def apply(inputs, weights):
        return convolve(inputs, weights, stride, pads)
    return jax.vjp(apply, field.astype(jnp.float32), kernel.astype(jnp.float32))

def reference(volume, kernel_one, kernel_two, kernel_three, kernel_four, cotangent):
    pre_one, pull_one = layer(volume, kernel_one, 2, (0, 1))
    act_one = jax.nn.silu(pre_one).astype(jnp.bfloat16)
    pre_two, pull_two = layer(act_one, kernel_two, 2, (0, 1))
    act_two = jax.nn.silu(pre_two).astype(jnp.bfloat16)
    pre_three, pull_three = layer(act_two, kernel_three, 1, (1, 1))
    act_three = jax.nn.silu(pre_three).astype(jnp.bfloat16)
    pre_four, pull_four = layer(act_three, kernel_four, 1, (1, 1))
    features = jax.nn.silu(pre_four).astype(jnp.bfloat16)
    back_four = (cotangent.astype(jnp.float32) * silu_slope(pre_four)).astype(jnp.bfloat16)
    into_three, grad_four = pull_four(back_four.astype(jnp.float32))
    back_three = (into_three * silu_slope(pre_three)).astype(jnp.bfloat16)
    into_two, grad_three = pull_three(back_three.astype(jnp.float32))
    back_two = (into_two * silu_slope(pre_two)).astype(jnp.bfloat16)
    into_one, grad_two = pull_two(back_two.astype(jnp.float32))
    back_one = (into_one * silu_slope(pre_one)).astype(jnp.bfloat16)
    unused, grad_one = pull_one(back_one.astype(jnp.float32))
    return (features, grad_one, grad_two, grad_three, grad_four)
```

```python
import functools

import jax
import jax.numpy as jnp
import numpy as np
from jax import lax
from jax.experimental import pallas as pl
from jax.experimental.pallas import tpu as pltpu
from jax.sharding import PartitionSpec as P

BF = jnp.bfloat16
F32 = jnp.float32
BOTH = ("space", "chan")
LANES = 128
VMEM_LIMIT = 48 * 1024 * 1024


def mm(left, right):
    return lax.dot_general(left, right, (((1,), (0,)), ((), ())), preferred_element_type=F32)


def mm_nt(left, right):
    return lax.dot_general(left, right, (((1,), (1,)), ((), ())), preferred_element_type=F32)


def lane_of(shape):
    return lax.broadcasted_iota(jnp.int32, shape, len(shape) - 1)


def shifted(value, step):
    width = value.shape[1]
    turned = pltpu.roll(value, step % width, 1)
    edge = 0 if step == 1 else LANES - 1
    return jnp.where(lane_of(value.shape) % LANES == edge, 0.0, turned)


def activate(pre):
    sigma = jax.nn.sigmoid(pre)
    return pre * sigma, sigma * (1.0 + pre * (1.0 - sigma))


def call(kernel, outs, args, scratch=(), flops=0):
    smem = pl.BlockSpec(memory_space=pltpu.SMEM)
    vmem = pl.BlockSpec(memory_space=pltpu.VMEM)
    size = sum(a.size * a.dtype.itemsize for a in args)
    size += sum(int(np.prod(s)) * jnp.dtype(t).itemsize for s, t in outs)
    return pl.pallas_call(
        kernel,
        out_shape=[jax.ShapeDtypeStruct(s, t) for s, t in outs],
        in_specs=[smem if a.dtype == jnp.int32 else vmem for a in args],
        out_specs=[vmem] * len(outs),
        scratch_shapes=[pltpu.VMEM(s, t) for s, t in scratch],
        compiler_params=pltpu.CompilerParams(vmem_limit_bytes=VMEM_LIMIT),
        cost_estimate=pl.CostEstimate(flops=flops, bytes_accessed=size, transcendentals=0),
    )(*args)


def first_layers_kernel(vol, phases, rows, w_one, w_two, field, act_one, slope_one, act_two, slope_two):
    for d in range(19):
        block = jnp.reshape(vol[:, d], (64, 512))
        split = mm(block, phases[...]).astype(BF)
        stacked = jnp.concatenate([split[:, p * 128 : p * 128 + 128] for p in range(5)], 0)
        field[d] = mm(rows[...], stacked).astype(BF)
    for d in range(9):
        columns = []
        for h in range(5):
            parts = [field[2 * d + a, h * 64 : h * 64 + 96] for a in range(3)]
            columns.append(jnp.concatenate(parts, 0))
        pre = mm(w_one[...], jnp.concatenate(columns, 1))
        act, slope = activate(pre)
        if d < 8:
            slope_one[d] = slope[:, :512]
        beside = shifted(act[:32], -1)
        for h in range(5):
            lanes = slice(h * 128, h * 128 + 128)
            act_one[d, h * 96 : h * 96 + 64] = act[:, lanes].astype(BF)
            act_one[d, h * 96 + 64 : h * 96 + 96] = beside[:, lanes].astype(BF)
    for d in range(4):
        columns = []
        for h in range(2):
            parts = [act_one[2 * d + a, h * 192 : h * 192 + 288] for a in range(3)]
            columns.append(jnp.concatenate(parts, 0))
        pre = mm(w_two[...], jnp.concatenate(columns, 1))
        act, slope = activate(pre)
        act_two[d] = act.astype(BF)
        slope_two[d] = slope


def taps_of(field, d, start, width):
    parts = []
    for a in range(3):
        for b in range(3):
            parts.append(field[d + a, :, pl.ds(start + b * LANES, width)])
    return jnp.concatenate(parts, 0)


def shift_sum(product, channels):
    low = product[:channels]
    mid = product[channels : 2 * channels]
    high = product[2 * channels :]
    return shifted(low, 1) + mid + shifted(high, -1)


def clear_rims(field):
    depth, channels, lanes = field.shape
    rim = jnp.zeros((depth, channels, LANES), BF)
    field[:, :, :LANES] = rim
    field[:, :, lanes - LANES :] = rim


def assemble(field, me, pieces, channels):
    clear_rims(field)
    for near, far in ((0, 1), (2, 3)):
        for k in (near, far):
            body, up, down = pieces[k]
            at = pl.multiple_of((me ^ k) * channels, channels)
            field[0, pl.ds(at, channels), LANES : 9 * LANES] = up
            for d in range(4):
                field[d + 1, pl.ds(at, channels), LANES : 9 * LANES] = body[d]
            field[5, pl.ds(at, channels), LANES : 9 * LANES] = down


def pieces_of(own, own_up, own_down, across, across_up, across_down, core, rest):
    return {
        0: (own, own_up[0], own_down[0]),
        2: (across, across_up[0], across_down[0]),
        1: (core, rest[4], rest[5]),
        3: (rest, rest[6], rest[7]),
    }


def third_kernel(me_ref, *refs):
    blocks, weights = refs[:8], refs[8]
    act, slope, field = refs[9:]
    me = me_ref[0]
    clear_rims(field)
    pieces = pieces_of(*blocks)
    for k in range(4):
        body, up, down = pieces[k]
        at = pl.multiple_of(LANES + (me ^ k) * (2 * LANES), LANES)
        lanes = pl.ds(at, 2 * LANES)
        field[0, :, lanes] = up
        for d in range(4):
            field[d + 1, :, lanes] = body[d]
        field[5, :, lanes] = down
    for d in range(4):
        product = mm(weights[...], taps_of(field, d, 0, 1024))
        value, steep = activate(shift_sum(product, 32))
        act[d] = value.astype(BF)
        slope[d] = steep


def fourth_kernel(me_ref, *refs):
    blocks, weights, cotangent = refs[:8], refs[8], refs[9]
    features, back, field = refs[10:]
    assemble(field, me_ref[0], pieces_of(*blocks), 32)
    for d in range(4):
        product = mm(weights[...], taps_of(field, d, 0, 1024))
        value, steep = activate(shift_sum(product, 64))
        features[d] = value.astype(BF)
        back[d] = (cotangent[d].astype(F32) * steep).astype(BF)


def flipped_weights(kernel):
    columns = []
    for a in range(3):
        for b in range(3):
            taps = [((2 - a) * 3 + 2 - b) * 3 + 2 - c for c in range(3)]
            columns.append(jnp.concatenate([kernel[t] for t in taps], 0))
    return jnp.concatenate(columns, 1)


def into_three_kernel(me_ref, *refs):
    blocks, kernel, slope = refs[:8], refs[8], refs[9]
    back, field = refs[10:]
    assemble(field, me_ref[0], pieces_of(*blocks), 64)
    weights = flipped_weights(kernel)
    for d in range(4):
        product = mm(weights, taps_of(field, d, 0, 1024))
        back[d] = (shift_sum(product, 32) * slope[d]).astype(BF)


def into_two_kernel(me_ref, *refs):
    blocks, kernel, slope = refs[:8], refs[8], refs[9]
    back, field = refs[10:]
    me = me_ref[0]
    assemble(field, me, pieces_of(*blocks), 32)
    weights = flipped_weights(kernel)
    start = pl.multiple_of(me * (2 * LANES), LANES)
    for d in range(4):
        product = mm(weights, taps_of(field, d, start, 2 * LANES))
        back[d] = (shift_sum(product, 64) * slope[d]).astype(BF)


def three_shifts(value):
    wide = value.astype(F32)
    return jnp.concatenate([shifted(wide, 1).astype(BF), value, shifted(wide, -1).astype(BF)], 0)


def filter_grad(wide, gradient, grad):
    total = None
    for d in range(4):
        term = mm_nt(taps_of(wide, d, 0, 1024), gradient[d + 1, :, LANES : 9 * LANES])
        total = term if total is None else total + term
    grad[...] = total.astype(grad.dtype)


def grad_four_kernel(own, up, down, gradient, grad, wide):
    clear_rims(wide)
    inside = slice(LANES, 9 * LANES)
    wide[0, :, inside] = three_shifts(up[0])
    for d in range(4):
        wide[d + 1, :, inside] = three_shifts(own[d])
    wide[5, :, inside] = three_shifts(down[0])
    filter_grad(wide, gradient, grad)


def grad_three_kernel(me_ref, field, gradient, grad, wide):
    clear_rims(wide)
    inside = slice(LANES, 9 * LANES)
    at = pl.multiple_of(me_ref[0] * 16, 16)
    for d in range(6):
        wide[d, :, inside] = three_shifts(field[d, pl.ds(at, 16), inside])
    filter_grad(wide, gradient, grad)


def last_kernel(back, plane, row, corner, act_one, slope_one, field, w_back, grads, wide, back_one):
    def place(d, h, value):
        wide[d, h, :64] = value
        wide[d, h, 64:] = shifted(value.astype(F32), 1).astype(BF)

    place(0, 0, corner[0])
    for h in range(2):
        place(0, h + 1, plane[0, :, h * 128 : h * 128 + 128])
    for d in range(4):
        place(d + 1, 0, row[d])
        for h in range(2):
            place(d + 1, h + 1, back[d, :, h * 128 : h * 128 + 128])
    for d_odd in range(2):
        for h_odd in range(2):
            taps = [(a, b) for a in ((1,) if d_odd else (0, 2)) for b in ((1,) if h_odd else (0, 2))]
            weights = jnp.concatenate([w_back[a * 3 + b] for a, b in taps], 1)
            columns = []
            for d in range(4):
                for h in range(2):
                    parts = [wide[d + 1 - a // 2, h + 1 - b // 2] for a, b in taps]
                    columns.append(jnp.concatenate(parts, 0))
            into = mm(weights, jnp.concatenate(columns, 1))
            for d in range(4):
                for h in range(2):
                    at = (d * 2 + h) * 128
                    lanes = slice((2 * h + h_odd) * 128, (2 * h + h_odd) * 128 + 128)
                    d_one = 2 * d + d_odd
                    value = into[:, at : at + 128] * slope_one[d_one, :, lanes]
                    back_one[d_one, :, lanes] = value.astype(BF)
    two = None
    for d in range(4):
        columns = []
        for h in range(2):
            parts = [act_one[2 * d + a, h * 192 : h * 192 + 288] for a in range(3)]
            columns.append(jnp.concatenate(parts, 0))
        term = mm_nt(jnp.concatenate(columns, 1), back[d])
        two = term if two is None else two + term
    one = None
    for d in range(8):
        columns = []
        for h in range(4):
            parts = [field[2 * d + a, h * 64 : h * 64 + 96] for a in range(3)]
            columns.append(jnp.concatenate(parts, 0))
        term = mm_nt(jnp.concatenate(columns, 1), back_one[d])
        one = term if one is None else one + term
    both = jnp.concatenate([two, one], 0)
    grads[:576] = jnp.concatenate([both[:576], both[576:]], 1)
    grads[576:] = jnp.zeros((448, 128), F32)


def moved(block, depth_step, chan_of):
    depth, chans = lax.axis_size("space"), lax.axis_size("chan")
    route = []
    for s in range(depth):
        for c in range(chans):
            to = chan_of(c)
            if 0 <= s + depth_step < depth and 0 <= to < chans:
                route.append((s * chans + c, (s + depth_step) * chans + to))
    return lax.ppermute(block, BOTH, route)


def gathered(own):
    first, last = own[:1], own[3:]
    across = moved(own, 0, lambda c: c ^ 2)
    own_up = moved(last, 1, lambda c: c)
    own_down = moved(first, -1, lambda c: c)
    across_up = moved(last, 1, lambda c: c ^ 2)
    across_down = moved(first, -1, lambda c: c ^ 2)
    core = moved(own, 0, lambda c: c ^ 1)
    rest = jnp.concatenate([across, own_up, own_down, across_up, across_down], 0)
    rest = moved(rest, 0, lambda c: c ^ 1)
    return [own, own_up, own_down, across, across_up, across_down, core, rest]


def summed(parts, axis):
    count = parts.shape[0]
    terms = lax.all_to_all(parts, axis, 0, 0)
    total = jnp.sum(terms.astype(F32), 0).astype(parts.dtype)
    return lax.all_to_all(jnp.broadcast_to(total[None], (count,) + total.shape), axis, 0, 0)


def phase_matrix():
    pick = np.zeros((512, 640), np.float32)
    for p in range(5):
        for w in range(128):
            if 4 * w + p < 512:
                pick[4 * w + p, p * 128 + w] = 1.0
    return jnp.asarray(pick, BF)


def row_matrix():
    pick = np.zeros((11, 8, 4, 5, 4, 16), np.float32)
    for h in range(11):
        for p in range(5):
            for i in range(4):
                pick[h, p, i, p, i, h] = 1.0
    return jnp.asarray(pick.reshape(352, 320), BF)


def per_device(volume, kernel_one, kernel_two, kernel_three, kernel_four, cotangent):
    me = lax.axis_index("chan").astype(jnp.int32)[None]
    below = moved(volume[:, :3], -1, lambda c: c)
    beside = moved(volume[:, :, :3], 0, lambda c: c - 1)
    corner = moved(volume[:, :3, :3], -1, lambda c: c - 1)
    tall = jnp.concatenate([volume, below], 1)
    side = jnp.pad(jnp.concatenate([beside, corner], 1), ((0, 0), (0, 0), (0, 5), (0, 0)))
    tall = jnp.concatenate([tall, side], 2)

    even = jnp.pad(kernel_one, ((0, 0), (0, 0), (0, 5), (0, 0), (0, 0)))
    odd = jnp.pad(kernel_one, ((0, 0), (0, 0), (2, 3), (0, 0), (0, 0)))
    w_one = jnp.stack([even, odd]).reshape(2, 288, 32).transpose(0, 2, 1).reshape(64, 288)
    w_two = kernel_two.reshape(864, 64).T
    field, act_one, slope_one, act_two, slope_two = call(
        first_layers_kernel,
        [((19, 352, 128), BF), ((9, 480, 128), BF), ((8, 64, 512), F32), ((4, 64, 256), BF), ((4, 64, 256), F32)],
        [tall, phase_matrix(), row_matrix(), w_one, w_two],
    )

    all_kernel_three = lax.all_gather(kernel_three, "chan", axis=3, tiled=True)
    mine = lax.dynamic_slice_in_dim(all_kernel_three, lax.axis_index("chan") * 32, 32, axis=4)
    w_three = jnp.transpose(mine, (2, 4, 0, 1, 3)).reshape(96, 576)
    mine = lax.all_to_all(kernel_four, "chan", split_axis=4, concat_axis=3, tiled=True)
    w_four = jnp.transpose(mine, (2, 4, 0, 1, 3)).reshape(192, 1152)
    cotangent = jnp.transpose(cotangent.reshape(64, 4, 1024), (1, 0, 2))

    act_three, slope_three, field_three = call(
        third_kernel,
        [((4, 32, 1024), BF), ((4, 32, 1024), F32), ((6, 64, 1280), BF)],
        [me, *gathered(act_two), w_three],
    )
    blocks = gathered(act_three)
    features, back_four = call(
        fourth_kernel,
        [((4, 64, 1024), BF), ((4, 64, 1024), BF)],
        [me, *blocks, w_four, cotangent],
        [((6, 128, 1280), BF)],
    )
    features = jnp.transpose(features, (1, 0, 2)).reshape(64, 4, 8, 128)
    back_three, all_four = call(
        into_three_kernel,
        [((4, 32, 1024), BF), ((6, 256, 1280), BF)],
        [me, *gathered(back_four), kernel_four.reshape(27, 32, 256), slope_three],
    )
    (grad_four,) = call(
        grad_four_kernel,
        [((864, 256), BF)],
        [*blocks[:3], all_four],
        [((6, 96, 1280), BF)],
        flops=2 * 864 * 256 * 4096,
    )
    back_two, all_three = call(
        into_two_kernel,
        [((4, 64, 256), BF), ((6, 128, 1280), BF)],
        [me, *gathered(back_three), all_kernel_three.reshape(27, 64, 128), slope_two],
    )
    (grad_three,) = call(
        grad_three_kernel,
        [((432, 128), BF)],
        [me, field_three, all_three],
        [((6, 48, 1280), BF)],
        flops=2 * 432 * 128 * 4096,
    )
    plane = moved(back_two[3:], 1, lambda c: c)
    row = moved(back_two[:, :, 128:], 0, lambda c: c + 1)
    corner = moved(back_two[3:, :, 128:], 1, lambda c: c + 1)
    top = jnp.concatenate([kernel_two[:, :, 0], kernel_two[:, :, 2]], 3)
    bottom = jnp.pad(kernel_two[:, :, 1], ((0, 0), (0, 0), (0, 0), (0, 64)))
    w_back = jnp.concatenate([top, bottom], 2).reshape(9, 64, 128)
    (grads,) = call(
        last_kernel,
        [((1024, 128), F32)],
        [back_two, plane, row, corner, act_one, slope_one, field, w_back],
        [((5, 3, 128, 128), BF), ((8, 64, 512), BF)],
    )
    grad_four = summed(grad_four.reshape(32, 27, 256), "space").astype(F32)
    grad_four = grad_four.reshape(3, 3, 3, 32, 256)
    grad_three = summed(grad_three.reshape(32, 27, 64), "space").astype(F32)
    grad_three = grad_three.reshape(3, 3, 3, 16, 128)
    grads = summed(grads.reshape(128, 8, 128), BOTH).reshape(1024, 128)
    grads = jnp.concatenate([grads[:576, :64], grads[:576, 64:]], 0)
    grad_two = grads[:864].reshape(3, 3, 3, 32, 64)
    phases = grads[864:].reshape(3, 3, 8, 4, 64)
    grad_one = phases[:, :, 0:3, :, :32] + phases[:, :, 2:5, :, 32:]
    return (features, grad_one, grad_two, grad_three, grad_four)


def solution(mesh):
    in_specs = (
        P(None, "space", "chan", None),
        P(),
        P(),
        P(None, None, None, "chan", None),
        P(None, None, None, "chan", None),
        P("chan", "space", None, None),
    )
    out_specs = (
        P("chan", "space", None, None),
        P(),
        P(),
        P(None, None, None, "chan", None),
        P(None, None, None, "chan", None),
    )
    return jax.shard_map(
        per_device, mesh=mesh, in_specs=in_specs, out_specs=out_specs, check_vma=False
    )
```

```python
import jax
import jax.numpy as jnp
import numpy as np
from jax import lax
from jax.experimental import pallas as pl
from jax.experimental.pallas import tpu as pltpu
from jax.sharding import PartitionSpec as P

BF = jnp.bfloat16
F32 = jnp.float32
BOTH = ("space", "chan")
LANES = 128
VMEM_LIMIT = 20 * 1024 * 1024


def mm(left, right):
    return lax.dot_general(left, right, (((1,), (0,)), ((), ())), preferred_element_type=F32)


def mm_nt(left, right):
    return lax.dot_general(left, right, (((1,), (1,)), ((), ())), preferred_element_type=F32)


def lane_of(shape):
    return lax.broadcasted_iota(jnp.int32, shape, len(shape) - 1)


def shifted(value, step):
    width = value.shape[1]
    turned = pltpu.roll(value, step % width, 1)
    edge = 0 if step == 1 else LANES - 1
    return jnp.where(lane_of(value.shape) % LANES == edge, 0.0, turned)


def activate(pre):
    sigma = jax.nn.sigmoid(pre)
    return pre * sigma, sigma * (1.0 + pre * (1.0 - sigma))


def call(kernel, outs, args, scratch=(), flops=0, anywhere=()):
    specs = []
    for place, a in enumerate(args):
        space = pltpu.SMEM if a.dtype == jnp.int32 else pltpu.VMEM
        specs.append(pl.BlockSpec(memory_space=pl.ANY if place in anywhere else space))
    size = sum(a.size * a.dtype.itemsize for a in args)
    size += sum(int(np.prod(s)) * jnp.dtype(t).itemsize for s, t in outs)
    buffers = [pltpu.VMEM(s, t) for s, t in scratch]
    if anywhere:
        buffers.append(pltpu.SemaphoreType.DMA((14,)))
    return pl.pallas_call(
        kernel,
        out_shape=[jax.ShapeDtypeStruct(s, t) for s, t in outs],
        in_specs=specs,
        out_specs=[pl.BlockSpec(memory_space=pltpu.VMEM)] * len(outs),
        scratch_shapes=buffers,
        compiler_params=pltpu.CompilerParams(vmem_limit_bytes=VMEM_LIMIT),
        cost_estimate=pl.CostEstimate(flops=flops, bytes_accessed=size, transcendentals=0),
    )(*args)


def first_layers_kernel(vol, phases, rows, w_one, w_two, field, act_one, slope_one, body, first, last, slope_two):
    for d in range(19):
        block = jnp.reshape(vol[:, d], (64, 512))
        split = mm(block, phases[...]).astype(BF)
        stacked = jnp.concatenate([split[:, p * 128 : p * 128 + 128] for p in range(5)], 0)
        field[d] = mm(rows[...], stacked).astype(BF)
    for d in range(9):
        columns = []
        for h in range(5):
            parts = [field[2 * d + a, h * 64 : h * 64 + 96] for a in range(3)]
            columns.append(jnp.concatenate(parts, 0))
        pre = mm(w_one[...], jnp.concatenate(columns, 1))
        act, slope = activate(pre)
        if d < 8:
            slope_one[d] = slope[:, :512]
        beside = shifted(act[:32], -1)
        for h in range(5):
            lanes = slice(h * 128, h * 128 + 128)
            act_one[d, h * 96 : h * 96 + 64] = act[:, lanes].astype(BF)
            act_one[d, h * 96 + 64 : h * 96 + 96] = beside[:, lanes].astype(BF)
    for d in range(4):
        columns = []
        for h in range(2):
            parts = [act_one[2 * d + a, h * 192 : h * 192 + 288] for a in range(3)]
            columns.append(jnp.concatenate(parts, 0))
        pre = mm(w_two[...], jnp.concatenate(columns, 1))
        act, slope = activate(pre)
        slope_two[d] = slope
        steep = slope.astype(BF)
        body[d, :, :256] = act.astype(BF)
        body[d, :, 256:] = steep[:, 128:]
        for rim, at in ((first, 0), (last, 3)):
            if d == at:
                rim[0, :, :256] = act.astype(BF)
                rim[0, :, 256:] = steep


def prepare_kernel(me_ref, packed, w_three, w_four, w_two_back):
    me = me_ref[0]

    def tap_of(t, four):
        if four:
            return jnp.concatenate([packed[j, t, :32] for j in range(4)], 0)
        return jnp.concatenate([packed[j, t, 32:, :128] for j in range(4)], 0)

    def own(count, wide):
        row = lax.broadcasted_iota(jnp.int32, (count, wide), 0)
        return jnp.where(lane_of((count, wide)) == row + me * count, 1.0, 0.0).astype(BF)

    for out, four, count in ((w_three, False, 32), (w_four, True, 64)):
        pick = own(count, 4 * count)
        for c in range(3):
            rows = jnp.concatenate([tap_of(ab * 3 + c, four) for ab in range(9)], 0)
            out[c * count : c * count + count] = mm_nt(pick, rows).astype(BF)
    w_two_back[...] = flipped_weights([tap_of(t, False) for t in range(27)])


def taps_of(field, d, start, width):
    parts = []
    for a in range(3):
        for b in range(3):
            parts.append(field[d + a, :, pl.ds(start + b * LANES, width)])
    return jnp.concatenate(parts, 0)


def shift_sum(product, channels):
    low = product[:channels]
    mid = product[channels : 2 * channels]
    high = product[2 * channels :]
    return shifted(low, 1) + mid + shifted(high, -1)


def clear_rims(field):
    depth, channels, lanes = field.shape
    rim = jnp.zeros((depth, channels, LANES), BF)
    field[:, :, :LANES] = rim
    field[:, :, lanes - LANES :] = rim


def arrive(refs, sems, target, up=1, width=1024):
    copies = []
    for k in range(4):
        body, rim = refs[2 * k], refs[2 * k + 1]
        lanes = pl.ds(0, width)
        sources = (body.at[:, :, lanes], rim.at[pl.ds(0, up), :, lanes], rim.at[pl.ds(up, 1), :, lanes])
        for piece, source in enumerate(sources):
            copies.append(pltpu.make_async_copy(source, target(k, piece), sems.at[3 * k + piece]))
    for copy in copies:
        copy.start()
    return copies


def assemble(field, me, refs, sems, channels, up=1, rim=1):
    planes = (pl.ds(up, 4), pl.ds(0, up), pl.ds(up + 4, 1))

    def target(k, piece):
        at = pl.multiple_of((me ^ k) * channels, channels)
        return field.at[planes[piece], pl.ds(at, channels), pl.ds(rim * LANES, 8 * LANES)]

    return arrive(refs, sems, target, up)


def third_kernel(me_ref, *refs):
    blocks, weights = refs[:8], refs[8]
    act, slope, field, steep_front, steep_row, sems = refs[9:]
    me = me_ref[0]
    planes = (pl.ds(1, 4), pl.ds(0, 1), pl.ds(5, 1))

    def target(k, piece):
        at = pl.multiple_of(LANES + (me ^ k) * (2 * LANES), LANES)
        return field.at[planes[piece], :, pl.ds(at, 2 * LANES)]

    copies = arrive(blocks, sems, target, 1, 2 * LANES)
    clear_rims(field)
    for copy in copies:
        copy.wait()

    @pl.when(me == 0)
    def _():
        steep_front[:, :LANES] = jnp.zeros((64, LANES), BF)
        steep_row[...] = jnp.zeros((4, 64, LANES), BF)

    plane = pltpu.make_async_copy(
        blocks[1].at[0, :, pl.ds(256, 256)], steep_front.at[:, pl.ds(LANES, 256)], sems.at[12]
    )
    plane.start()
    plane.wait()
    for k in (1, 3):

        @pl.when((me > 0) & (me ^ k == me - 1))
        def _(k=k):
            corner = pltpu.make_async_copy(
                blocks[2 * k + 1].at[0, :, pl.ds(384, LANES)], steep_front.at[:, pl.ds(0, LANES)], sems.at[12]
            )
            row = pltpu.make_async_copy(blocks[2 * k].at[:, :, pl.ds(256, LANES)], steep_row, sems.at[13])
            corner.start()
            row.start()
            corner.wait()
            row.wait()

    for d in range(4):
        product = mm(weights[...], taps_of(field, d, 0, 1024))
        value, steep = activate(shift_sum(product, 32))
        act[d] = value.astype(BF)
        slope[d] = steep


def fourth_kernel(me_ref, *refs):
    blocks, weights, cotangent = refs[:8], refs[8], refs[9]
    features, back, field, sems = refs[10:]
    copies = assemble(field, me_ref[0], blocks, sems, 32)
    clear_rims(field)
    for copy in copies:
        copy.wait()
    for d in range(4):
        product = mm(weights[...], taps_of(field, d, 0, 1024))
        value, steep = activate(shift_sum(product, 64))
        features[d] = value.astype(BF)
        back[d] = (cotangent[d].astype(F32) * steep).astype(BF)


def flipped_weights(kernel):
    columns = []
    for a in range(3):
        for b in range(3):
            taps = [((2 - a) * 3 + 2 - b) * 3 + 2 - c for c in range(3)]
            columns.append(jnp.concatenate([kernel[t] for t in taps], 0))
    return jnp.concatenate(columns, 1)


def into_three_kernel(me_ref, *refs):
    blocks, kernel, slope = refs[:8], refs[8], refs[9]
    back, field, sems = refs[10:]
    copies = assemble(field, me_ref[0], blocks, sems, 64)
    clear_rims(field)
    weights = flipped_weights(kernel)
    for copy in copies:
        copy.wait()
    for d in range(4):
        product = mm(weights, taps_of(field, d, 0, 1024))
        back[d] = (shift_sum(product, 32) * slope[d]).astype(BF)


def three_shifts(value):
    wide = value.astype(F32)
    return jnp.concatenate([shifted(wide, 1).astype(BF), value, shifted(wide, -1).astype(BF)], 0)


def filter_grad(wide, gradient, first, rim):
    total = None
    for d in range(4):
        own = gradient[d + first, :, rim * LANES : (rim + 8) * LANES]
        term = mm_nt(taps_of(wide, d, 0, 1024), own)
        total = term if total is None else total + term
    return total


def grad_four_kernel(own, rim, gradient, grad, wide):
    clear_rims(wide)
    inside = slice(LANES, 9 * LANES)
    wide[0, :, inside] = three_shifts(rim[0])
    for d in range(4):
        wide[d + 1, :, inside] = three_shifts(own[d])
    wide[5, :, inside] = three_shifts(rim[1])
    grad[...] = filter_grad(wide, gradient, 1, 1).astype(BF)


def last_kernel(me_ref, *refs):
    blocks = refs[:8]
    weights, slope, front, row, act_one, slope_one, volume, w_back, act_two, grad_four = refs[8:18]
    out, field, shifts, wide, back_one, sems = refs[18:]
    me = me_ref[0]
    copies = assemble(field, me, blocks, sems, 32, up=2, rim=2)
    field[:, :, : 2 * LANES] = jnp.zeros((7, 128, 2 * LANES), BF)
    field[:, :, 10 * LANES :] = jnp.zeros((7, 128, LANES), BF)
    clear_rims(shifts)
    inside = slice(LANES, 9 * LANES)
    channels = pl.ds(pl.multiple_of(me * 16, 16), 16)
    for d in range(6):
        shifts[d, :, inside] = three_shifts(act_two[d, channels, inside])
    for t in range(27):
        out[t, :32] = grad_four[t]
    for t in range(27, 32):
        out[t] = jnp.zeros((48, 256), BF)
    for copy in copies:
        copy.wait()

    start = pl.multiple_of(me * (2 * LANES), LANES)
    for d in range(5):
        steep = front[...].astype(F32)
        if d > 0:
            steep = jnp.concatenate([row[d - 1].astype(F32), slope[d - 1]], 1)
        product = mm(weights[...], taps_of(field, d, start, 3 * LANES))
        value = shift_sum(product, 64) * steep
        value = value.astype(BF)
        beside = shifted(value.astype(F32), 1).astype(BF)
        for h in range(3):
            wide[d, h, :64] = value[:, h * 128 : h * 128 + 128]
            wide[d, h, 64:] = beside[:, h * 128 : h * 128 + 128]
    for d_odd in range(2):
        for h_odd in range(2):
            taps = [(a, b) for a in ((1,) if d_odd else (0, 2)) for b in ((1,) if h_odd else (0, 2))]
            mixed = jnp.concatenate([w_back[a * 3 + b] for a, b in taps], 1)
            columns = []
            for d in range(4):
                for h in range(2):
                    parts = [wide[d + 1 - a // 2, h + 1 - b // 2] for a, b in taps]
                    columns.append(jnp.concatenate(parts, 0))
            into = mm(mixed, jnp.concatenate(columns, 1))
            for d in range(4):
                for h in range(2):
                    at = (d * 2 + h) * 128
                    lanes = slice((2 * h + h_odd) * 128, (2 * h + h_odd) * 128 + 128)
                    d_one = 2 * d + d_odd
                    value = into[:, at : at + 128] * slope_one[d_one, :, lanes]
                    back_one[d_one, :, lanes] = value.astype(BF)
    three = filter_grad(shifts, field, 2, 2).astype(BF)
    for t in range(27):
        out[t, 32:, :128] = three[t * 16 : t * 16 + 16]
    two = None
    for d in range(4):
        columns = []
        for h in range(2):
            parts = [act_one[2 * d + a, h * 192 : h * 192 + 288] for a in range(3)]
            columns.append(jnp.concatenate(parts, 0))
        own = jnp.concatenate([wide[d + 1, 1, :64], wide[d + 1, 2, :64]], 1)
        term = mm_nt(jnp.concatenate(columns, 1), own)
        two = term if two is None else two + term
    one = None
    for d in range(8):
        columns = []
        for h in range(4):
            parts = [volume[2 * d + a, h * 64 : h * 64 + 96] for a in range(3)]
            columns.append(jnp.concatenate(parts, 0))
        term = mm_nt(jnp.concatenate(columns, 1), back_one[d])
        one = term if one is None else one + term
    both = jnp.concatenate([two, one], 0)
    for t in range(32):
        pair = [both[32 * t + 16 * q : 32 * t + 16 * q + 16] for q in range(2)]
        out[t, 32:, 128:] = jnp.concatenate(pair, 1).astype(BF)
    rest = [both[1024 + 32 * q : 1056 + 32 * q] for q in range(4)]
    out[27, :32] = jnp.concatenate(rest, 1).astype(BF)


def unpack_kernel(packed, grad_one, grad_two, grad_three, grad_four, both):
    for t in range(27):
        grad_four[t] = packed[t, :32].astype(F32)
        grad_three[t] = packed[t, 32:, :128].astype(F32)
    for t in range(32):
        pair = packed[t, 32:, 128:].astype(F32)
        both[32 * t : 32 * t + 16] = pair[:, :64]
        both[32 * t + 16 : 32 * t + 32] = pair[:, 64:]
    rest = packed[27, :32].astype(F32)
    for q in range(4):
        both[1024 + 32 * q : 1056 + 32 * q] = rest[:, 64 * q : 64 * q + 64]
    grad_two[...] = both[:864]
    for t in range(9):
        at = 864 + 32 * t
        grad_one[t] = both[at : at + 12, :32] + both[at + 8 : at + 20, 32:]


def moved(block, depth_step, chan_of):
    depth, chans = lax.axis_size("space"), lax.axis_size("chan")
    route = []
    for s in range(depth):
        for c in range(chans):
            to = chan_of(c)
            if 0 <= s + depth_step < depth and 0 <= to < chans:
                route.append((s * chans + c, (s + depth_step) * chans + to))
    return lax.ppermute(block, BOTH, route)


def gathered(own, first, last):
    across = moved(own, 0, lambda c: c ^ 2)
    up = moved(last, 1, lambda c: c)
    down = moved(first, -1, lambda c: c)
    core = moved(own, 0, lambda c: c ^ 1)
    rim = jnp.concatenate([up, down], 0)
    across_rim = moved(rim, 0, lambda c: c ^ 2)
    core_rim = moved(rim, 0, lambda c: c ^ 1)
    across, across_rim = lax.optimization_barrier((across, across_rim))
    last_pair = [moved(piece, 0, lambda c: c ^ 1) for piece in (across, across_rim)]
    return [own, rim, core, core_rim, across, across_rim, *last_pair]


def summed(parts):
    terms = lax.all_to_all(parts, "space", 0, 0)
    own = jnp.sum(terms.astype(F32), 0)
    sent = own.astype(BF)
    others = [moved(sent, 0, lambda c, k=k: c ^ k).astype(F32) for k in (2, 3, 1)]
    shape = own.shape
    row = lax.broadcasted_iota(jnp.int32, shape, 0)
    shared = (row >= 32) & (lane_of(shape) >= 128) | (lax.axis_index("space") == 27)
    total = own + jnp.where(shared, others[0] + others[1] + others[2], 0.0)
    total = total.astype(BF)
    return lax.all_to_all(jnp.broadcast_to(total[None], parts.shape), "space", 0, 0)


def phase_matrix():
    pick = np.zeros((512, 640), np.float32)
    for p in range(5):
        for w in range(128):
            if 4 * w + p < 512:
                pick[4 * w + p, p * 128 + w] = 1.0
    return jnp.asarray(pick, BF)


def row_matrix():
    pick = np.zeros((11, 8, 4, 5, 4, 16), np.float32)
    for h in range(11):
        for p in range(5):
            for i in range(4):
                pick[h, p, i, p, i, h] = 1.0
    return jnp.asarray(pick.reshape(352, 320), BF)


def per_device(volume, kernel_one, kernel_two, kernel_three, kernel_four, cotangent):
    me = lax.axis_index("chan").astype(jnp.int32)[None]
    below = moved(volume[:, :3], -1, lambda c: c)
    beside = moved(volume[:, :, :3], 0, lambda c: c - 1)
    corner = moved(volume[:, :3, :3], -1, lambda c: c - 1)
    tall = jnp.concatenate([volume, below], 1)
    side = jnp.pad(jnp.concatenate([beside, corner], 1), ((0, 0), (0, 0), (0, 5), (0, 0)))
    tall = jnp.concatenate([tall, side], 2)

    three = jnp.pad(kernel_three.reshape(27, 16, 128), ((0, 0), (0, 0), (0, 128)))
    four = kernel_four.reshape(27, 32, 256)
    filters = lax.all_gather(jnp.concatenate([four, three], 1), "chan")
    cotangent = jnp.transpose(cotangent.reshape(64, 4, 1024), (1, 0, 2))

    even = jnp.pad(kernel_one, ((0, 0), (0, 0), (0, 5), (0, 0), (0, 0)))
    odd = jnp.pad(kernel_one, ((0, 0), (0, 0), (2, 3), (0, 0), (0, 0)))
    w_one = jnp.stack([even, odd]).reshape(2, 288, 32).transpose(0, 2, 1).reshape(64, 288)
    w_two = kernel_two.reshape(864, 64).T
    top = jnp.concatenate([kernel_two[:, :, 0], kernel_two[:, :, 2]], 3)
    bottom = jnp.pad(kernel_two[:, :, 1], ((0, 0), (0, 0), (0, 0), (0, 64)))
    w_back = jnp.concatenate([top, bottom], 2).reshape(9, 64, 128)

    field, act_one, slope_one, body, first, last, slope_two = call(
        first_layers_kernel,
        [
            ((19, 352, 128), BF),
            ((9, 480, 128), BF),
            ((8, 64, 512), F32),
            ((4, 64, 384), BF),
            ((1, 64, 512), BF),
            ((1, 64, 512), BF),
            ((4, 64, 256), F32),
        ],
        [tall, phase_matrix(), row_matrix(), w_one, w_two],
    )
    w_three, w_four, w_two_back = call(
        prepare_kernel,
        [((96, 576), BF), ((192, 1152), BF), ((192, 1152), BF)],
        [me, filters],
    )
    pieces = range(1, 9)
    act_three, slope_three, field_three, front, row = call(
        third_kernel,
        [((4, 32, 1024), BF), ((4, 32, 1024), F32), ((6, 64, 1280), BF), ((64, 384), BF), ((4, 64, 128), BF)],
        [me, *gathered(body, first, last), w_three],
        anywhere=pieces,
    )
    blocks = gathered(act_three, act_three[:1], act_three[3:])
    features, back_four = call(
        fourth_kernel,
        [((4, 64, 1024), BF), ((4, 64, 1024), BF)],
        [me, *blocks, w_four, cotangent],
        [((6, 128, 1280), BF)],
        anywhere=pieces,
    )
    features = jnp.transpose(features, (1, 0, 2)).reshape(64, 4, 8, 128)
    back_three, all_four = call(
        into_three_kernel,
        [((4, 32, 1024), BF), ((6, 256, 1280), BF)],
        [me, *gathered(back_four, back_four[:1], back_four[3:]), four, slope_three],
        anywhere=pieces,
    )
    (grad_four,) = call(
        grad_four_kernel,
        [((864, 256), BF)],
        [*blocks[:2], all_four],
        [((6, 96, 1280), BF)],
        flops=2 * 864 * 256 * 4096,
    )
    (grads,) = call(
        last_kernel,
        [((32, 48, 256), BF)],
        [
            me,
            *gathered(back_three, back_three[:1], back_three[2:]),
            w_two_back,
            slope_two,
            front,
            row,
            act_one,
            slope_one,
            field,
            w_back,
            field_three,
            grad_four.reshape(27, 32, 256),
        ],
        [
            ((7, 128, 1408), BF),
            ((6, 48, 1280), BF),
            ((5, 3, 128, 128), BF),
            ((8, 64, 512), BF),
        ],
        anywhere=pieces,
    )
    grad_one, grad_two, grad_three, grad_four = call(
        unpack_kernel,
        [((9, 12, 32), F32), ((864, 64), F32), ((27, 16, 128), F32), ((27, 32, 256), F32)],
        [summed(grads)],
        [((1152, 64), F32)],
    )
    grad_one = grad_one.reshape(3, 3, 3, 4, 32)
    grad_two = grad_two.reshape(3, 3, 3, 32, 64)
    grad_three = grad_three.reshape(3, 3, 3, 16, 128)
    grad_four = grad_four.reshape(3, 3, 3, 32, 256)
    return (features, grad_one, grad_two, grad_three, grad_four)


def solution(mesh):
    in_specs = (
        P(None, "space", "chan", None),
        P(),
        P(),
        P(None, None, None, "chan", None),
        P(None, None, None, "chan", None),
        P("chan", "space", None, None),
    )
    out_specs = (
        P("chan", "space", None, None),
        P(),
        P(),
        P(None, None, None, "chan", None),
        P(None, None, None, "chan", None),
    )
    return jax.shard_map(
        per_device, mesh=mesh, in_specs=in_specs, out_specs=out_specs, check_vma=False
    )
```

```python
import jax
import jax.numpy as jnp
import numpy as np
from jax import lax
from jax.experimental import pallas as pl
from jax.experimental.pallas import tpu as pltpu
from jax.sharding import PartitionSpec as P

BF = jnp.bfloat16
F32 = jnp.float32
BOTH = ("space", "chan")
LANES = 128
VMEM_LIMIT = 20 * 1024 * 1024


def mm(left, right):
    return lax.dot_general(left, right, (((1,), (0,)), ((), ())), preferred_element_type=F32)


def mm_nt(left, right):
    return lax.dot_general(left, right, (((1,), (1,)), ((), ())), preferred_element_type=F32)


def lane_of(shape):
    return lax.broadcasted_iota(jnp.int32, shape, len(shape) - 1)


def shifted(value, step):
    width = value.shape[1]
    turned = pltpu.roll(value, step % width, 1)
    edge = 0 if step == 1 else LANES - 1
    return jnp.where(lane_of(value.shape) % LANES == edge, 0.0, turned)


def activate(pre):
    sigma = jax.nn.sigmoid(pre)
    return pre * sigma, sigma * (1.0 + pre * (1.0 - sigma))


def call(kernel, outs, args, scratch=(), flops=0, anywhere=(), away=(), far=()):
    specs = []
    for place, a in enumerate(args):
        space = pltpu.SMEM if a.dtype == jnp.int32 else pltpu.VMEM
        specs.append(pl.BlockSpec(memory_space=pl.ANY if place in anywhere else space))
    size = sum(a.size * a.dtype.itemsize for a in args)
    args = [pltpu.with_memory_space_constraint(a, pltpu.HBM) if place in far else a for place, a in enumerate(args)]
    size += sum(int(np.prod(s)) * jnp.dtype(t).itemsize for s, t in outs)
    buffers = [pltpu.VMEM(s, t) for s, t in scratch]
    buffers.append(pltpu.SemaphoreType.DMA((20,)))
    places = [pltpu.HBM if place in away else pltpu.VMEM for place in range(len(outs))]
    return pl.pallas_call(
        kernel,
        out_shape=[
            pltpu.HBM(s, t) if place in away else jax.ShapeDtypeStruct(s, t)
            for place, (s, t) in enumerate(outs)
        ],
        in_specs=specs,
        out_specs=[pl.BlockSpec(memory_space=place) for place in places],
        scratch_shapes=buffers,
        compiler_params=pltpu.CompilerParams(vmem_limit_bytes=VMEM_LIMIT),
        cost_estimate=pl.CostEstimate(flops=flops, bytes_accessed=size, transcendentals=0),
    )(*args)


def begin(source, target, sem):
    copy = pltpu.make_async_copy(source, target, sem)
    copy.start()
    return copy


def picks(shape, column_of):
    row = lax.broadcasted_iota(jnp.int32, shape, 0)
    return jnp.where(column_of(row, lane_of(shape)), 1.0, 0.0).astype(BF)


def phase_matrix():
    return picks((512, 640), lambda row, lane: row == 4 * (lane % 128) + lane // 128)


def row_matrix():
    def at(row, lane):
        return lane == row // 4 % 8 * 64 + row % 4 * 16 + row // 32

    return picks((352, 320), at)


def first_layers_kernel(vol, w_one, w_two, *refs):
    field_out, act_one_out, slope_one_out, body, first, last, slope_two = refs[:7]
    field, act_one, slope_one, sems = refs[7:]
    phases = phase_matrix()
    rows = row_matrix()
    for d in range(19):
        block = jnp.reshape(vol[:, d], (64, 512))
        split = mm(block, phases).astype(BF)
        stacked = jnp.concatenate([split[:, p * 128 : p * 128 + 128] for p in range(5)], 0)
        field[d] = mm(rows, stacked).astype(BF)
    leaving = [begin(field, field_out, sems.at[0])]
    for d in range(9):
        columns = []
        for h in range(5):
            parts = [field[2 * d + a, h * 64 : h * 64 + 96] for a in range(3)]
            columns.append(jnp.concatenate(parts, 0))
        pre = mm(w_one[...], jnp.concatenate(columns, 1))
        act, slope = activate(pre)
        if d < 8:
            slope_one[d] = slope[:, :512]
        beside = shifted(act[:32], -1)
        for h in range(5):
            lanes = slice(h * 128, h * 128 + 128)
            act_one[d, h * 96 : h * 96 + 64] = act[:, lanes].astype(BF)
            act_one[d, h * 96 + 64 : h * 96 + 96] = beside[:, lanes].astype(BF)
    leaving.append(begin(slope_one, slope_one_out, sems.at[1]))
    leaving.append(begin(act_one, act_one_out, sems.at[2]))
    for d in range(4):
        columns = []
        for h in range(2):
            parts = [act_one[2 * d + a, h * 192 : h * 192 + 288] for a in range(3)]
            columns.append(jnp.concatenate(parts, 0))
        pre = mm(w_two[...], jnp.concatenate(columns, 1))
        act, slope = activate(pre)
        slope_two[d] = slope
        steep = slope.astype(BF)
        body[d, :, :256] = act.astype(BF)
        body[d, :, 256:] = steep[:, 128:]
        for rim, at in ((first, 0), (last, 3)):
            if d == at:
                rim[0, :, :256] = act.astype(BF)
                rim[0, :, 256:] = steep
    for copy in leaving:
        copy.wait()


def turned(me, blocks, count):
    wide = 4 * count
    row = lax.broadcasted_iota(jnp.int32, (count, wide), 0)
    pick = jnp.where(lane_of((count, wide)) == row + me * count, 1.0, 0.0).astype(BF)
    parts = []
    for c in range(3):
        rows = [blocks[j, ab * 3 + c] for ab in range(9) for j in range(4)]
        parts.append(mm_nt(pick, jnp.concatenate(rows, 0)).astype(BF))
    return jnp.concatenate(parts, 0)


def taps_of(field, d, start, width):
    parts = []
    for a in range(3):
        for b in range(3):
            parts.append(field[d + a, :, pl.ds(start + b * LANES, width)])
    return jnp.concatenate(parts, 0)


def shift_sum(product, channels):
    low = product[:channels]
    mid = product[channels : 2 * channels]
    high = product[2 * channels :]
    return shifted(low, 1) + mid + shifted(high, -1)


def clear_rims(field):
    depth, channels, lanes = field.shape
    rim = jnp.zeros((depth, channels, LANES), BF)
    field[:, :, :LANES] = rim
    field[:, :, lanes - LANES :] = rim


def arrive(refs, sems, target, up=1, width=1024):
    copies = []
    for k in range(4):
        body, rim = refs[2 * k], refs[2 * k + 1]
        lanes = pl.ds(0, width)
        sources = (body.at[:, :, lanes], rim.at[pl.ds(0, up), :, lanes], rim.at[pl.ds(up, 1), :, lanes])
        for piece, source in enumerate(sources):
            copies.append(pltpu.make_async_copy(source, target(k, piece), sems.at[3 * k + piece]))
    for copy in copies:
        copy.start()
    return copies


def assemble(field, me, refs, sems, channels, up=1, rim=1):
    planes = (pl.ds(up, 4), pl.ds(0, up), pl.ds(up + 4, 1))

    def target(k, piece):
        at = pl.multiple_of((me ^ k) * channels, channels)
        return field.at[planes[piece], pl.ds(at, channels), pl.ds(rim * LANES, 8 * LANES)]

    return arrive(refs, sems, target, up)


def third_kernel(me_ref, *refs):
    blocks, filters = refs[:8], refs[8]
    act, first, last, slope_out, own_out, front_out, row_out = refs[9:16]
    field, slope, front, row, kernel, sems = refs[16:]
    me = me_ref[0]
    arrived = begin(filters.at[:, :, pl.ds(32, 16), pl.ds(0, LANES)], kernel, sems.at[12])
    planes = (pl.ds(1, 4), pl.ds(0, 1), pl.ds(5, 1))

    def target(k, piece):
        at = pl.multiple_of(LANES + (me ^ k) * (2 * LANES), LANES)
        return field.at[planes[piece], :, pl.ds(at, 2 * LANES)]

    copies = arrive(blocks, sems, target, 1, 2 * LANES)
    plane = begin(blocks[1].at[0, :, pl.ds(256, 256)], front.at[:, pl.ds(LANES, 256)], sems.at[13])

    @pl.when(me == 0)
    def _():
        front[:, :LANES] = jnp.zeros((64, LANES), BF)
        row[...] = jnp.zeros((4, 64, LANES), BF)

    for k in (1, 3):

        @pl.when((me > 0) & (me ^ k == me - 1))
        def _(k=k):
            begin(blocks[2 * k + 1].at[0, :, pl.ds(384, LANES)], front.at[:, pl.ds(0, LANES)], sems.at[14])
            begin(blocks[2 * k].at[:, :, pl.ds(256, LANES)], row, sems.at[15])

    clear_rims(field)
    arrived.wait()
    weights = turned(me, kernel, 32)
    plane.wait()

    @pl.when(me > 0)
    def _():
        corner = blocks[1].at[0, :, pl.ds(384, LANES)]
        pltpu.make_async_copy(corner, front.at[:, pl.ds(0, LANES)], sems.at[14]).wait()
        pltpu.make_async_copy(blocks[0].at[:, :, pl.ds(256, LANES)], row, sems.at[15]).wait()

    leaving = [begin(front, front_out, sems.at[16]), begin(row, row_out, sems.at[17])]
    for copy in copies:
        copy.wait()
    own = field.at[:, pl.ds(pl.multiple_of(me * 16, 16), 16), :]
    leaving.append(begin(own, own_out, sems.at[18]))
    for d in range(4):
        product = mm(weights, taps_of(field, d, 0, 1024))
        value, steep = activate(shift_sum(product, 32))
        act[d] = value.astype(BF)
        slope[d] = steep
    first[0] = act[0]
    last[0] = act[3]
    leaving.append(begin(slope, slope_out, sems.at[19]))
    for copy in leaving:
        copy.wait()


def fourth_kernel(me_ref, *refs):
    blocks, filters, cotangent = refs[:8], refs[8], refs[9]
    features, back, first, last, field, kernel, sems = refs[10:]
    me = me_ref[0]
    arrived = begin(filters.at[:, :, pl.ds(0, 32), :], kernel, sems.at[12])
    copies = assemble(field, me, blocks, sems, 32)
    clear_rims(field)
    arrived.wait()
    weights = turned(me, kernel, 64)
    for copy in copies:
        copy.wait()
    for d in range(4):
        product = mm(weights, taps_of(field, d, 0, 1024))
        value, steep = activate(shift_sum(product, 64))
        features[d] = value.astype(BF)
        back[d] = (cotangent[d].astype(F32) * steep).astype(BF)
    first[0] = back[0]
    last[0] = back[3]


def flipped_weights(kernel):
    columns = []
    for a in range(3):
        for b in range(3):
            taps = [((2 - a) * 3 + 2 - b) * 3 + 2 - c for c in range(3)]
            columns.append(jnp.concatenate([kernel[t] for t in taps], 0))
    return jnp.concatenate(columns, 1)


def into_three_kernel(me_ref, *refs):
    blocks, kernel, steep = refs[:8], refs[8], refs[9]
    back, first, last, field, slope, sems = refs[10:]
    copies = assemble(field, me_ref[0], blocks, sems, 64)
    copies.append(begin(steep, slope, sems.at[12]))
    clear_rims(field)
    weights = flipped_weights(kernel)
    for copy in copies:
        copy.wait()
    for d in range(4):
        product = mm(weights, taps_of(field, d, 0, 1024))
        back[d] = (shift_sum(product, 32) * slope[d]).astype(BF)
    first[0] = back[0]
    last[...] = back[2:]


def three_shifts(value):
    wide = value.astype(F32)
    return jnp.concatenate([shifted(wide, 1).astype(BF), value, shifted(wide, -1).astype(BF)], 0)


def filter_grad(wide, gradients):
    total = None
    for d in range(4):
        term = mm_nt(taps_of(wide, d, 0, 1024), gradients(d))
        total = term if total is None else total + term
    return total


def grad_four_kernel(me_ref, own, rim, *refs):
    blocks, grad, wide, gradient, sems = refs[:4], *refs[4:]
    copies = []
    for k in range(4):
        at = pl.multiple_of((me_ref[0] ^ k) * 64, 64)
        copies.append(begin(blocks[k], gradient.at[:, pl.ds(at, 64), :], sems.at[k]))
    clear_rims(wide)
    inside = slice(LANES, 9 * LANES)
    wide[0, :, inside] = three_shifts(rim[0])
    for d in range(4):
        wide[d + 1, :, inside] = three_shifts(own[d])
    wide[5, :, inside] = three_shifts(rim[1])
    for copy in copies:
        copy.wait()
    grad[...] = filter_grad(wide, lambda d: gradient[d]).astype(BF)


def last_kernel(me_ref, *refs):
    blocks = refs[:8]
    filters, w_back, act_two, grad_four = refs[8:12]
    away, out, field, shifts, wide, back_one, kernel = refs[12:18], *refs[18:24]
    slope, front, row, act_one, slope_one, volume = refs[24:30]
    sems = refs[30]
    me = me_ref[0]
    arrived = begin(filters.at[:, :, pl.ds(32, 16), pl.ds(0, LANES)], kernel, sems.at[12])
    copies = assemble(field, me, blocks, sems, 32, up=2, rim=2)
    later = [begin(source, refs[24 + n], sems.at[13 + n]) for n, source in enumerate(away)]
    field[:, :, : 2 * LANES] = jnp.zeros((7, 128, 2 * LANES), BF)
    field[:, :, 10 * LANES :] = jnp.zeros((7, 128, LANES), BF)
    clear_rims(shifts)
    inside = slice(LANES, 9 * LANES)
    for d in range(6):
        shifts[d, :, inside] = three_shifts(act_two[d, :, inside])
    for t in range(27):
        out[t, :32] = grad_four[t]
    for t in range(27, 32):
        out[t] = jnp.zeros((48, 256), BF)
    arrived.wait()
    taps = [jnp.concatenate([kernel[j, t] for j in range(4)], 0) for t in range(27)]
    weights = flipped_weights(taps)
    for copy in copies + later:
        copy.wait()

    start = pl.multiple_of(me * (2 * LANES), LANES)
    for d in range(5):
        steep = front[...].astype(F32)
        if d > 0:
            steep = jnp.concatenate([row[d - 1].astype(F32), slope[d - 1]], 1)
        product = mm(weights, taps_of(field, d, start, 3 * LANES))
        value = shift_sum(product, 64) * steep
        value = value.astype(BF)
        beside = shifted(value.astype(F32), 1).astype(BF)
        for h in range(3):
            wide[d, h, :64] = value[:, h * 128 : h * 128 + 128]
            wide[d, h, 64:] = beside[:, h * 128 : h * 128 + 128]
    for d_odd in range(2):
        for h_odd in range(2):
            taps = [(a, b) for a in ((1,) if d_odd else (0, 2)) for b in ((1,) if h_odd else (0, 2))]
            mixed = jnp.concatenate([w_back[a * 3 + b] for a, b in taps], 1)
            columns = []
            for d in range(4):
                for h in range(2):
                    parts = [wide[d + 1 - a // 2, h + 1 - b // 2] for a, b in taps]
                    columns.append(jnp.concatenate(parts, 0))
            into = mm(mixed, jnp.concatenate(columns, 1))
            for d in range(4):
                for h in range(2):
                    at = (d * 2 + h) * 128
                    lanes = slice((2 * h + h_odd) * 128, (2 * h + h_odd) * 128 + 128)
                    d_one = 2 * d + d_odd
                    value = into[:, at : at + 128] * slope_one[d_one, :, lanes]
                    back_one[d_one, :, lanes] = value.astype(BF)
    three = filter_grad(shifts, lambda d: field[d + 2, :, 2 * LANES : 10 * LANES]).astype(BF)
    for t in range(27):
        out[t, 32:, :128] = three[t * 16 : t * 16 + 16]
    two = None
    for d in range(4):
        columns = []
        for h in range(2):
            parts = [act_one[2 * d + a, h * 192 : h * 192 + 288] for a in range(3)]
            columns.append(jnp.concatenate(parts, 0))
        own = jnp.concatenate([wide[d + 1, 1, :64], wide[d + 1, 2, :64]], 1)
        term = mm_nt(jnp.concatenate(columns, 1), own)
        two = term if two is None else two + term
    one = None
    for d in range(8):
        columns = []
        for h in range(4):
            parts = [volume[2 * d + a, h * 64 : h * 64 + 96] for a in range(3)]
            columns.append(jnp.concatenate(parts, 0))
        term = mm_nt(jnp.concatenate(columns, 1), back_one[d])
        one = term if one is None else one + term
    both = jnp.concatenate([two, one], 0)
    for t in range(32):
        pair = [both[32 * t + 16 * q : 32 * t + 16 * q + 16] for q in range(2)]
        out[t, 32:, 128:] = jnp.concatenate(pair, 1).astype(BF)
    rest = [both[1024 + 32 * q : 1056 + 32 * q] for q in range(4)]
    out[27, :32] = jnp.concatenate(rest, 1).astype(BF)


def unpack_kernel(packed, grad_one, grad_two, grad_three, grad_four, both, sems):
    for t in range(27):
        grad_four[t] = packed[t, :32].astype(F32)
        grad_three[t] = packed[t, 32:, :128].astype(F32)
    for t in range(32):
        pair = packed[t, 32:, 128:].astype(F32)
        both[32 * t : 32 * t + 16] = pair[:, :64]
        both[32 * t + 16 : 32 * t + 32] = pair[:, 64:]
    rest = packed[27, :32].astype(F32)
    for q in range(4):
        both[1024 + 32 * q : 1056 + 32 * q] = rest[:, 64 * q : 64 * q + 64]
    grad_two[...] = both[:864]
    for t in range(9):
        at = 864 + 32 * t
        grad_one[t] = both[at : at + 12, :32] + both[at + 8 : at + 20, 32:]


def moved(block, depth_step, chan_of):
    depth, chans = lax.axis_size("space"), lax.axis_size("chan")
    route = []
    for s in range(depth):
        for c in range(chans):
            to = chan_of(c)
            if 0 <= s + depth_step < depth and 0 <= to < chans:
                route.append((s * chans + c, (s + depth_step) * chans + to))
    return lax.ppermute(block, BOTH, route)


def gathered(own, first, last):
    across = moved(own, 0, lambda c: c ^ 2)
    up = moved(last, 1, lambda c: c)
    down = moved(first, -1, lambda c: c)
    core = moved(own, 0, lambda c: c ^ 1)
    rim = jnp.concatenate([up, down], 0)
    across_rim = moved(rim, 0, lambda c: c ^ 2)
    core_rim = moved(rim, 0, lambda c: c ^ 1)
    across, across_rim = lax.optimization_barrier((across, across_rim))
    last_pair = [moved(piece, 0, lambda c: c ^ 1) for piece in (across, across_rim)]
    return [own, rim, core, core_rim, across, across_rim, *last_pair]


def summed(parts):
    terms = lax.all_to_all(parts, "space", 0, 0)
    own = jnp.sum(terms.astype(F32), 0)
    sent = own.astype(BF)
    others = [moved(sent, 0, lambda c, k=k: c ^ k).astype(F32) for k in (2, 3, 1)]
    shape = own.shape
    row = lax.broadcasted_iota(jnp.int32, shape, 0)
    shared = (row >= 32) & (lane_of(shape) >= 128) | (lax.axis_index("space") == 27)
    total = own + jnp.where(shared, others[0] + others[1] + others[2], 0.0)
    total = total.astype(BF)
    return lax.all_to_all(jnp.broadcast_to(total[None], parts.shape), "space", 0, 0)


def per_device(volume, kernel_one, kernel_two, kernel_three, kernel_four, cotangent):
    me = lax.axis_index("chan").astype(jnp.int32)[None]
    below = moved(volume[:, :3], -1, lambda c: c)
    beside = moved(volume[:, :, :3], 0, lambda c: c - 1)
    corner = moved(volume[:, :3, :3], -1, lambda c: c - 1)

    three = jnp.pad(kernel_three.reshape(27, 16, 128), ((0, 0), (0, 0), (0, 128)))
    four = kernel_four.reshape(27, 32, 256)
    filters = lax.all_gather(jnp.concatenate([four, three], 1), "chan")
    cotangent = jnp.transpose(cotangent.reshape(64, 4, 1024), (1, 0, 2))
    corner, cotangent = lax.optimization_barrier((corner, cotangent))

    even = jnp.pad(kernel_one, ((0, 0), (0, 0), (0, 5), (0, 0), (0, 0)))
    odd = jnp.pad(kernel_one, ((0, 0), (0, 0), (2, 3), (0, 0), (0, 0)))
    w_one = jnp.stack([even, odd]).reshape(2, 288, 32).transpose(0, 2, 1).reshape(64, 288)
    w_two = kernel_two.reshape(864, 64).T
    top = jnp.concatenate([kernel_two[:, :, 0], kernel_two[:, :, 2]], 3)
    bottom = jnp.pad(kernel_two[:, :, 1], ((0, 0), (0, 0), (0, 0), (0, 64)))
    w_back = jnp.concatenate([top, bottom], 2).reshape(9, 64, 128)

    tall = jnp.concatenate([volume, below], 1)
    side = jnp.pad(jnp.concatenate([beside, corner], 1), ((0, 0), (0, 0), (0, 5), (0, 0)))
    tall = jnp.concatenate([tall, side], 2)

    field, act_one, slope_one, body, first, last, slope_two = call(
        first_layers_kernel,
        [
            ((19, 352, 128), BF),
            ((9, 480, 128), BF),
            ((8, 64, 512), F32),
            ((4, 64, 384), BF),
            ((1, 64, 512), BF),
            ((1, 64, 512), BF),
            ((4, 64, 256), F32),
        ],
        [tall, w_one, w_two],
        [((19, 352, 128), BF), ((9, 480, 128), BF), ((8, 64, 512), F32)],
        away=(0, 1, 2),
    )
    pieces = range(1, 10)
    act_three, first, last, slope_three, own_two, front, row = call(
        third_kernel,
        [((4, 32, 1024), BF), ((1, 32, 1024), BF), ((1, 32, 1024), BF), ((4, 32, 1024), F32), ((6, 16, 1280), BF), ((64, 384), BF), ((4, 64, 128), BF)],
        [me, *gathered(body, first, last), filters],
        [((6, 64, 1280), BF), ((4, 32, 1024), F32), ((64, 384), BF), ((4, 64, 128), BF), ((4, 27, 16, 128), BF)],
        anywhere=pieces,
        away=(3, 4, 5, 6),
        far=(9,),
    )
    blocks = gathered(act_three, first, last)
    features, back_four, first, last = call(
        fourth_kernel,
        [((4, 64, 1024), BF), ((4, 64, 1024), BF), ((1, 64, 1024), BF), ((1, 64, 1024), BF)],
        [me, *blocks, filters, cotangent],
        [((6, 128, 1280), BF), ((4, 27, 32, 256), BF)],
        anywhere=pieces,
    )
    features = jnp.transpose(features, (1, 0, 2)).reshape(64, 4, 8, 128)
    all_four = gathered(back_four, first, last)
    back_three, first, last = call(
        into_three_kernel,
        [((4, 32, 1024), BF), ((1, 32, 1024), BF), ((2, 32, 1024), BF)],
        [me, *all_four, four, slope_three],
        [((6, 256, 1280), BF), ((4, 32, 1024), F32)],
        anywhere=[*range(1, 9), 10],
    )
    (grad_four,) = call(
        grad_four_kernel,
        [((864, 256), BF)],
        [me, *blocks[:2], *all_four[::2]],
        [((6, 96, 1280), BF), ((4, 256, 1024), BF)],
        flops=2 * 864 * 256 * 4096,
        anywhere=range(3, 7),
    )
    (grads,) = call(
        last_kernel,
        [((32, 48, 256), BF)],
        [
            me,
            *gathered(back_three, first, last),
            filters,
            w_back,
            own_two,
            grad_four.reshape(27, 32, 256),
            slope_two,
            front,
            row,
            act_one,
            slope_one,
            field,
        ],
        [
            ((7, 128, 1408), BF),
            ((6, 48, 1280), BF),
            ((5, 3, 128, 128), BF),
            ((8, 64, 512), BF),
            ((4, 27, 16, 128), BF),
            ((4, 64, 256), F32),
            ((64, 384), BF),
            ((4, 64, 128), BF),
            ((9, 480, 128), BF),
            ((8, 64, 512), F32),
            ((19, 352, 128), BF),
        ],
        anywhere=[*range(1, 10), *range(13, 19)],
    )
    grad_one, grad_two, grad_three, grad_four = call(
        unpack_kernel,
        [((9, 12, 32), F32), ((864, 64), F32), ((27, 16, 128), F32), ((27, 32, 256), F32)],
        [summed(grads)],
        [((1152, 64), F32)],
    )
    grad_one = grad_one.reshape(3, 3, 3, 4, 32)
    grad_two = grad_two.reshape(3, 3, 3, 32, 64)
    grad_three = grad_three.reshape(3, 3, 3, 16, 128)
    grad_four = grad_four.reshape(3, 3, 3, 32, 256)
    return (features, grad_one, grad_two, grad_three, grad_four)


def solution(mesh):
    in_specs = (
        P(None, "space", "chan", None),
        P(),
        P(),
        P(None, None, None, "chan", None),
        P(None, None, None, "chan", None),
        P("chan", "space", None, None),
    )
    out_specs = (
        P("chan", "space", None, None),
        P(),
        P(),
        P(None, None, None, "chan", None),
        P(None, None, None, "chan", None),
    )
    return jax.shard_map(
        per_device, mesh=mesh, in_specs=in_specs, out_specs=out_specs, check_vma=False
    )
```

```python
import jax
import jax.numpy as jnp
import numpy as np
from jax import lax
from jax.experimental import pallas as pl
from jax.experimental.pallas import tpu as pltpu
from jax.sharding import PartitionSpec as P

BF = jnp.bfloat16
F32 = jnp.float32
BOTH = ("space", "chan")
LANES = 128
VMEM_LIMIT = 20 * 1024 * 1024


def mm(left, right):
    return lax.dot_general(left, right, (((1,), (0,)), ((), ())), preferred_element_type=F32)


def mm_nt(left, right):
    return lax.dot_general(left, right, (((1,), (1,)), ((), ())), preferred_element_type=F32)


def lane_of(shape):
    return lax.broadcasted_iota(jnp.int32, shape, len(shape) - 1)


def shifted(value, step):
    width = value.shape[1]
    turned = pltpu.roll(value, step % width, 1)
    edge = 0 if step == 1 else LANES - 1
    return jnp.where(lane_of(value.shape) % LANES == edge, 0.0, turned)


def activate(pre):
    sigma = jax.nn.sigmoid(pre)
    return pre * sigma, sigma * (1.0 + pre * (1.0 - sigma))


def call(kernel, outs, args, scratch=(), flops=0, anywhere=(), away=(), far=()):
    specs = []
    for place, a in enumerate(args):
        space = pltpu.SMEM if a.dtype == jnp.int32 else pltpu.VMEM
        specs.append(pl.BlockSpec(memory_space=pl.ANY if place in anywhere else space))
    size = sum(a.size * a.dtype.itemsize for a in args)
    args = [pltpu.with_memory_space_constraint(a, pltpu.HBM) if place in far else a for place, a in enumerate(args)]
    size += sum(int(np.prod(s)) * jnp.dtype(t).itemsize for s, t in outs)
    buffers = [pltpu.VMEM(s, t) for s, t in scratch]
    buffers.append(pltpu.SemaphoreType.DMA((20,)))
    places = [pltpu.HBM if place in away else pltpu.VMEM for place in range(len(outs))]
    return pl.pallas_call(
        kernel,
        out_shape=[
            pltpu.HBM(s, t) if place in away else jax.ShapeDtypeStruct(s, t)
            for place, (s, t) in enumerate(outs)
        ],
        in_specs=specs,
        out_specs=[pl.BlockSpec(memory_space=place) for place in places],
        scratch_shapes=buffers,
        compiler_params=pltpu.CompilerParams(vmem_limit_bytes=VMEM_LIMIT),
        cost_estimate=pl.CostEstimate(flops=flops, bytes_accessed=size, transcendentals=0),
    )(*args)


def begin(source, target, sem):
    copy = pltpu.make_async_copy(source, target, sem)
    copy.start()
    return copy


def picks(shape, column_of):
    row = lax.broadcasted_iota(jnp.int32, shape, 0)
    return jnp.where(column_of(row, lane_of(shape)), 1.0, 0.0).astype(BF)


def phase_matrix():
    return picks((512, 640), lambda row, lane: row == 4 * (lane % 128) + lane // 128)


def row_matrix():
    def at(row, lane):
        return lane == row // 4 % 8 * 64 + row % 4 * 16 + row // 32

    return picks((352, 320), at)


def first_layers_kernel(vol, w_one, w_two, *refs):
    field_out, act_one_out, slope_one_out, body, first, last, slope_two = refs[:7]
    field, act_one, slope_one, sems = refs[7:]
    phases = phase_matrix()
    rows = row_matrix()
    for start in range(0, 19, 4):
        planes = range(start, min(start + 4, 19))
        block = jnp.concatenate([jnp.reshape(vol[:, d], (64, 512)) for d in planes], 0)
        split = mm(block, phases).astype(BF)
        columns = []
        for n in range(len(planes)):
            parts = [split[n * 64 : n * 64 + 64, p * 128 : p * 128 + 128] for p in range(5)]
            columns.append(jnp.concatenate(parts, 0))
        placed = mm(rows, jnp.concatenate(columns, 1)).astype(BF)
        for n, d in enumerate(planes):
            field[d] = placed[:, n * 128 : n * 128 + 128]
    leaving = [begin(field, field_out, sems.at[0])]
    for d in range(9):
        columns = []
        for h in range(5):
            parts = [field[2 * d + a, h * 64 : h * 64 + 96] for a in range(3)]
            columns.append(jnp.concatenate(parts, 0))
        pre = mm(w_one[...], jnp.concatenate(columns, 1))
        act, slope = activate(pre)
        if d < 8:
            slope_one[d] = slope[:, :512]
        beside = shifted(act[:32], -1)
        for h in range(5):
            lanes = slice(h * 128, h * 128 + 128)
            act_one[d, h * 96 : h * 96 + 64] = act[:, lanes].astype(BF)
            act_one[d, h * 96 + 64 : h * 96 + 96] = beside[:, lanes].astype(BF)
    leaving.append(begin(slope_one, slope_one_out, sems.at[1]))
    leaving.append(begin(act_one, act_one_out, sems.at[2]))
    for d in range(4):
        columns = []
        for h in range(2):
            parts = [act_one[2 * d + a, h * 192 : h * 192 + 288] for a in range(3)]
            columns.append(jnp.concatenate(parts, 0))
        pre = mm(w_two[...], jnp.concatenate(columns, 1))
        act, slope = activate(pre)
        slope_two[d] = slope
        steep = slope.astype(BF)
        body[d, :, :256] = act.astype(BF)
        body[d, :, 256:] = steep[:, 128:]
        for rim, at in ((first, 0), (last, 3)):
            if d == at:
                rim[0, :, :256] = act.astype(BF)
                rim[0, :, 256:] = steep
    for copy in leaving:
        copy.wait()


def turned(me, blocks, count):
    wide = 4 * count
    row = lax.broadcasted_iota(jnp.int32, (count, wide), 0)
    pick = jnp.where(lane_of((count, wide)) == row + me * count, 1.0, 0.0).astype(BF)
    parts = []
    for c in range(3):
        rows = [blocks[j, ab * 3 + c] for ab in range(9) for j in range(4)]
        parts.append(mm_nt(pick, jnp.concatenate(rows, 0)).astype(BF))
    return jnp.concatenate(parts, 0)


def taps_of(field, d, start, width):
    parts = []
    for a in range(3):
        for b in range(3):
            parts.append(field[d + a, :, pl.ds(start + b * LANES, width)])
    return jnp.concatenate(parts, 0)


def shift_sum(product, channels):
    low = product[:channels]
    mid = product[channels : 2 * channels]
    high = product[2 * channels :]
    return shifted(low, 1) + mid + shifted(high, -1)


def clear_rims(field):
    depth, channels, lanes = field.shape
    rim = jnp.zeros((depth, channels, LANES), BF)
    field[:, :, :LANES] = rim
    field[:, :, lanes - LANES :] = rim


def arrive(refs, sems, target, up=1, width=1024):
    copies = []
    for k in range(4):
        body, rim = refs[2 * k], refs[2 * k + 1]
        lanes = pl.ds(0, width)
        sources = (body.at[:, :, lanes], rim.at[pl.ds(0, up), :, lanes], rim.at[pl.ds(up, 1), :, lanes])
        for piece, source in enumerate(sources):
            copies.append(pltpu.make_async_copy(source, target(k, piece), sems.at[3 * k + piece]))
    for copy in copies:
        copy.start()
    return copies


def assemble(field, me, refs, sems, channels, up=1, rim=1):
    planes = (pl.ds(up, 4), pl.ds(0, up), pl.ds(up + 4, 1))

    def target(k, piece):
        at = pl.multiple_of((me ^ k) * channels, channels)
        return field.at[planes[piece], pl.ds(at, channels), pl.ds(rim * LANES, 8 * LANES)]

    return arrive(refs, sems, target, up)


def third_kernel(me_ref, *refs):
    blocks, filters = refs[:8], refs[8]
    act, first, last, slope_out, own_out, front_out, row_out = refs[9:16]
    field, slope, front, row, kernel, sems = refs[16:]
    me = me_ref[0]
    arrived = begin(filters.at[:, :, pl.ds(32, 16), pl.ds(0, LANES)], kernel, sems.at[12])
    planes = (pl.ds(1, 4), pl.ds(0, 1), pl.ds(5, 1))

    def target(k, piece):
        at = pl.multiple_of(LANES + (me ^ k) * (2 * LANES), LANES)
        return field.at[planes[piece], :, pl.ds(at, 2 * LANES)]

    copies = arrive(blocks, sems, target, 1, 2 * LANES)
    plane = begin(blocks[1].at[0, :, pl.ds(256, 256)], front.at[:, pl.ds(LANES, 256)], sems.at[13])

    @pl.when(me == 0)
    def _():
        front[:, :LANES] = jnp.zeros((64, LANES), BF)
        row[...] = jnp.zeros((4, 64, LANES), BF)

    for k in (1, 3):

        @pl.when((me > 0) & (me ^ k == me - 1))
        def _(k=k):
            begin(blocks[2 * k + 1].at[0, :, pl.ds(384, LANES)], front.at[:, pl.ds(0, LANES)], sems.at[14])
            begin(blocks[2 * k].at[:, :, pl.ds(256, LANES)], row, sems.at[15])

    clear_rims(field)
    arrived.wait()
    weights = turned(me, kernel, 32)
    plane.wait()

    @pl.when(me > 0)
    def _():
        corner = blocks[1].at[0, :, pl.ds(384, LANES)]
        pltpu.make_async_copy(corner, front.at[:, pl.ds(0, LANES)], sems.at[14]).wait()
        pltpu.make_async_copy(blocks[0].at[:, :, pl.ds(256, LANES)], row, sems.at[15]).wait()

    leaving = [begin(front, front_out, sems.at[16]), begin(row, row_out, sems.at[17])]
    for copy in copies:
        copy.wait()
    own = field.at[:, pl.ds(pl.multiple_of(me * 16, 16), 16), :]
    leaving.append(begin(own, own_out, sems.at[18]))
    for d in range(4):
        product = mm(weights, taps_of(field, d, 0, 1024))
        value, steep = activate(shift_sum(product, 32))
        act[d] = value.astype(BF)
        slope[d] = steep
    first[0] = act[0]
    last[0] = act[3]
    leaving.append(begin(slope, slope_out, sems.at[19]))
    for copy in leaving:
        copy.wait()


def fourth_kernel(me_ref, *refs):
    blocks, filters, cotangent = refs[:8], refs[8], refs[9]
    features, back, first, last, field, kernel, sems = refs[10:]
    me = me_ref[0]
    arrived = begin(filters.at[:, :, pl.ds(0, 32), :], kernel, sems.at[12])
    copies = assemble(field, me, blocks, sems, 32)
    clear_rims(field)
    arrived.wait()
    weights = turned(me, kernel, 64)
    for copy in copies:
        copy.wait()
    for d in range(4):
        product = mm(weights, taps_of(field, d, 0, 1024))
        value, steep = activate(shift_sum(product, 64))
        features[d] = value.astype(BF)
        back[d] = (cotangent[d].astype(F32) * steep).astype(BF)
    first[0] = back[0]
    last[0] = back[3]


def flipped_weights(kernel):
    columns = []
    for a in range(3):
        for b in range(3):
            taps = [((2 - a) * 3 + 2 - b) * 3 + 2 - c for c in range(3)]
            columns.append(jnp.concatenate([kernel[t] for t in taps], 0))
    return jnp.concatenate(columns, 1)


def into_three_kernel(me_ref, *refs):
    blocks, kernel, steep = refs[:8], refs[8], refs[9]
    back, first, last, field, slope, sems = refs[10:]
    copies = assemble(field, me_ref[0], blocks, sems, 64)
    copies.append(begin(steep, slope, sems.at[12]))
    clear_rims(field)
    weights = flipped_weights(kernel)
    for copy in copies:
        copy.wait()
    for d in range(4):
        product = mm(weights, taps_of(field, d, 0, 1024))
        back[d] = (shift_sum(product, 32) * slope[d]).astype(BF)
    first[0] = back[0]
    last[...] = back[2:]


def three_shifts(value):
    wide = value.astype(F32)
    return jnp.concatenate([shifted(wide, 1).astype(BF), value, shifted(wide, -1).astype(BF)], 0)


def filter_grad(wide, gradients):
    total = None
    for d in range(4):
        term = mm_nt(taps_of(wide, d, 0, 1024), gradients(d))
        total = term if total is None else total + term
    return total


def grad_four_kernel(me_ref, own, rim, *refs):
    blocks, grad, wide, gradient, sems = refs[:4], *refs[4:]
    copies = []
    for k in range(4):
        at = pl.multiple_of((me_ref[0] ^ k) * 64, 64)
        copies.append(begin(blocks[k], gradient.at[:, pl.ds(at, 64), :], sems.at[k]))
    clear_rims(wide)
    inside = slice(LANES, 9 * LANES)
    wide[0, :, inside] = three_shifts(rim[0])
    for d in range(4):
        wide[d + 1, :, inside] = three_shifts(own[d])
    wide[5, :, inside] = three_shifts(rim[1])
    for copy in copies:
        copy.wait()
    grad[...] = filter_grad(wide, lambda d: gradient[d]).astype(BF)


def last_kernel(me_ref, *refs):
    blocks = refs[:8]
    filters, w_back, act_two, grad_four = refs[8:12]
    away, out, field, shifts, wide, back_one, kernel = refs[12:18], *refs[18:24]
    slope, front, row, act_one, slope_one, volume = refs[24:30]
    sems = refs[30]
    me = me_ref[0]
    arrived = begin(filters.at[:, :, pl.ds(32, 16), pl.ds(0, LANES)], kernel, sems.at[12])
    copies = assemble(field, me, blocks, sems, 32, up=2, rim=2)
    later = [begin(source, refs[24 + n], sems.at[13 + n]) for n, source in enumerate(away)]
    field[:, :, : 2 * LANES] = jnp.zeros((7, 128, 2 * LANES), BF)
    field[:, :, 10 * LANES :] = jnp.zeros((7, 128, LANES), BF)
    clear_rims(shifts)
    inside = slice(LANES, 9 * LANES)
    for d in range(6):
        shifts[d, :, inside] = three_shifts(act_two[d, :, inside])
    for t in range(27):
        out[t, :32] = grad_four[t]
    for t in range(27, 32):
        out[t] = jnp.zeros((48, 256), BF)
    arrived.wait()
    taps = [jnp.concatenate([kernel[j, t] for j in range(4)], 0) for t in range(27)]
    weights = flipped_weights(taps)
    for copy in copies + later:
        copy.wait()

    start = pl.multiple_of(me * (2 * LANES), LANES)
    for d in range(5):
        steep = front[...].astype(F32)
        if d > 0:
            steep = jnp.concatenate([row[d - 1].astype(F32), slope[d - 1]], 1)
        product = mm(weights, taps_of(field, d, start, 3 * LANES))
        value = shift_sum(product, 64) * steep
        value = value.astype(BF)
        beside = shifted(value.astype(F32), 1).astype(BF)
        for h in range(3):
            wide[d, h, :64] = value[:, h * 128 : h * 128 + 128]
            wide[d, h, 64:] = beside[:, h * 128 : h * 128 + 128]
    for d_odd in range(2):
        for h_odd in range(2):
            taps = [(a, b) for a in ((1,) if d_odd else (0, 2)) for b in ((1,) if h_odd else (0, 2))]
            mixed = jnp.concatenate([w_back[a * 3 + b] for a, b in taps], 1)
            columns = []
            for d in range(4):
                for h in range(2):
                    parts = [wide[d + 1 - a // 2, h + 1 - b // 2] for a, b in taps]
                    columns.append(jnp.concatenate(parts, 0))
            into = mm(mixed, jnp.concatenate(columns, 1))
            for d in range(4):
                for h in range(2):
                    at = (d * 2 + h) * 128
                    lanes = slice((2 * h + h_odd) * 128, (2 * h + h_odd) * 128 + 128)
                    d_one = 2 * d + d_odd
                    value = into[:, at : at + 128] * slope_one[d_one, :, lanes]
                    back_one[d_one, :, lanes] = value.astype(BF)
    three = filter_grad(shifts, lambda d: field[d + 2, :, 2 * LANES : 10 * LANES]).astype(BF)
    for t in range(27):
        out[t, 32:, :128] = three[t * 16 : t * 16 + 16]
    two = None
    for d in range(4):
        columns = []
        for h in range(2):
            parts = [act_one[2 * d + a, h * 192 : h * 192 + 288] for a in range(3)]
            columns.append(jnp.concatenate(parts, 0))
        own = jnp.concatenate([wide[d + 1, 1, :64], wide[d + 1, 2, :64]], 1)
        term = mm_nt(jnp.concatenate(columns, 1), own)
        two = term if two is None else two + term
    one = None
    for d in range(8):
        columns = []
        for h in range(4):
            parts = [volume[2 * d + a, h * 64 : h * 64 + 96] for a in range(3)]
            columns.append(jnp.concatenate(parts, 0))
        term = mm_nt(jnp.concatenate(columns, 1), back_one[d])
        one = term if one is None else one + term
    both = jnp.concatenate([two, one], 0)
    for t in range(32):
        pair = [both[32 * t + 16 * q : 32 * t + 16 * q + 16] for q in range(2)]
        out[t, 32:, 128:] = jnp.concatenate(pair, 1).astype(BF)
    rest = [both[1024 + 32 * q : 1056 + 32 * q] for q in range(4)]
    out[27, :32] = jnp.concatenate(rest, 1).astype(BF)


def unpack_kernel(packed, grad_one, grad_two, grad_three, grad_four, both, sems):
    for t in range(27):
        grad_four[t] = packed[t, :32].astype(F32)
        grad_three[t] = packed[t, 32:, :128].astype(F32)
    for t in range(32):
        pair = packed[t, 32:, 128:].astype(F32)
        both[32 * t : 32 * t + 16] = pair[:, :64]
        both[32 * t + 16 : 32 * t + 32] = pair[:, 64:]
    rest = packed[27, :32].astype(F32)
    for q in range(4):
        both[1024 + 32 * q : 1056 + 32 * q] = rest[:, 64 * q : 64 * q + 64]
    grad_two[...] = both[:864]
    for t in range(9):
        at = 864 + 32 * t
        value = both[at : at + 12, :32] + both[at + 8 : at + 20, 32:]
        for c in range(3):
            grad_one[t // 3, t % 3, c] = value[4 * c : 4 * c + 4]


def moved(block, depth_step, chan_of):
    depth, chans = lax.axis_size("space"), lax.axis_size("chan")
    route = []
    for s in range(depth):
        for c in range(chans):
            to = chan_of(c)
            if 0 <= s + depth_step < depth and 0 <= to < chans:
                route.append((s * chans + c, (s + depth_step) * chans + to))
    return lax.ppermute(block, BOTH, route)


def gathered(own, first, last, meanwhile=None):
    across = moved(own, 0, lambda c: c ^ 2)
    up = moved(last, 1, lambda c: c)
    down = moved(first, -1, lambda c: c)
    core = moved(own, 0, lambda c: c ^ 1)
    rim = jnp.concatenate([up, down], 0)
    across_rim = moved(rim, 0, lambda c: c ^ 2)
    core_rim = moved(rim, 0, lambda c: c ^ 1)
    across, across_rim, meanwhile = lax.optimization_barrier((across, across_rim, meanwhile))
    last_pair = [moved(piece, 0, lambda c: c ^ 1) for piece in (across, across_rim)]
    blocks = [own, rim, core, core_rim, across, across_rim, *last_pair]
    return blocks if meanwhile is None else (blocks, meanwhile)


def summed(parts):
    terms = lax.all_to_all(parts, "space", 0, 0)
    own = jnp.sum(terms.astype(F32), 0)
    shape = own.shape
    row = lax.broadcasted_iota(jnp.int32, shape, 0)
    shared = (row >= 32) & (lane_of(shape) >= 128) | (lax.axis_index("space") == 27)
    both = own
    for step in (1, 2):
        sent = lax.optimization_barrier(both.astype(BF))
        both = sent.astype(F32) + moved(sent, 0, lambda c, step=step: c ^ step).astype(F32)
    total = jnp.where(shared, both, own).astype(BF)
    return lax.all_to_all(jnp.broadcast_to(total[None], parts.shape), "space", 0, 0)


def per_device(volume, kernel_one, kernel_two, kernel_three, kernel_four, cotangent):
    me = lax.axis_index("chan").astype(jnp.int32)[None]
    below = moved(volume[:, :3], -1, lambda c: c)
    beside = moved(volume[:, :, :3], 0, lambda c: c - 1)
    corner = moved(volume[:, :3, :3], -1, lambda c: c - 1)

    three = jnp.pad(kernel_three.reshape(27, 16, 128), ((0, 0), (0, 0), (0, 128)))
    four = kernel_four.reshape(27, 32, 256)
    filters = lax.all_gather(jnp.concatenate([four, three], 1), "chan")
    cotangent = jnp.transpose(cotangent.reshape(64, 4, 1024), (1, 0, 2))
    corner, cotangent = lax.optimization_barrier((corner, cotangent))

    even = jnp.pad(kernel_one, ((0, 0), (0, 0), (0, 5), (0, 0), (0, 0)))
    odd = jnp.pad(kernel_one, ((0, 0), (0, 0), (2, 3), (0, 0), (0, 0)))
    w_one = jnp.stack([even, odd]).reshape(2, 288, 32).transpose(0, 2, 1).reshape(64, 288)
    w_two = kernel_two.reshape(864, 64).T
    top = jnp.concatenate([kernel_two[:, :, 0], kernel_two[:, :, 2]], 3)
    bottom = jnp.pad(kernel_two[:, :, 1], ((0, 0), (0, 0), (0, 0), (0, 64)))
    w_back = jnp.concatenate([top, bottom], 2).reshape(9, 64, 128)

    tall = jnp.concatenate([volume, below], 1)
    side = jnp.pad(jnp.concatenate([beside, corner], 1), ((0, 0), (0, 0), (0, 5), (0, 0)))
    tall = jnp.concatenate([tall, side], 2)

    field, act_one, slope_one, body, first, last, slope_two = call(
        first_layers_kernel,
        [
            ((19, 352, 128), BF),
            ((9, 480, 128), BF),
            ((8, 64, 512), F32),
            ((4, 64, 384), BF),
            ((1, 64, 512), BF),
            ((1, 64, 512), BF),
            ((4, 64, 256), F32),
        ],
        [tall, w_one, w_two],
        [((19, 352, 128), BF), ((9, 480, 128), BF), ((8, 64, 512), F32)],
        away=(0, 1, 2),
    )
    pieces = range(1, 10)
    act_three, first, last, slope_three, own_two, front, row = call(
        third_kernel,
        [((4, 32, 1024), BF), ((1, 32, 1024), BF), ((1, 32, 1024), BF), ((4, 32, 1024), F32), ((6, 16, 1280), BF), ((64, 384), BF), ((4, 64, 128), BF)],
        [me, *gathered(body, first, last), filters],
        [((6, 64, 1280), BF), ((4, 32, 1024), F32), ((64, 384), BF), ((4, 64, 128), BF), ((4, 27, 16, 128), BF)],
        anywhere=pieces,
        away=(3, 4, 5, 6),
        far=(9,),
    )
    blocks = gathered(act_three, first, last)
    features, back_four, first, last = call(
        fourth_kernel,
        [((4, 64, 1024), BF), ((4, 64, 1024), BF), ((1, 64, 1024), BF), ((1, 64, 1024), BF)],
        [me, *blocks, filters, cotangent],
        [((6, 128, 1280), BF), ((4, 27, 32, 256), BF)],
        anywhere=pieces,
    )
    features = jnp.transpose(features, (1, 0, 2)).reshape(64, 4, 8, 128)
    all_four = gathered(back_four, first, last)
    back_three, first, last = call(
        into_three_kernel,
        [((4, 32, 1024), BF), ((1, 32, 1024), BF), ((2, 32, 1024), BF)],
        [me, *all_four, four, slope_three],
        [((6, 256, 1280), BF), ((4, 32, 1024), F32)],
        anywhere=[*range(1, 9), 10],
    )
    (grad_four,) = call(
        grad_four_kernel,
        [((864, 256), BF)],
        [me, *blocks[:2], *all_four[::2]],
        [((6, 96, 1280), BF), ((4, 256, 1024), BF)],
        flops=2 * 864 * 256 * 4096,
        anywhere=range(3, 7),
    )
    blocks, grad_four = gathered(back_three, first, last, grad_four)
    (grads,) = call(
        last_kernel,
        [((32, 48, 256), BF)],
        [
            me,
            *blocks,
            filters,
            w_back,
            own_two,
            grad_four.reshape(27, 32, 256),
            slope_two,
            front,
            row,
            act_one,
            slope_one,
            field,
        ],
        [
            ((7, 128, 1408), BF),
            ((6, 48, 1280), BF),
            ((5, 3, 128, 128), BF),
            ((8, 64, 512), BF),
            ((4, 27, 16, 128), BF),
            ((4, 64, 256), F32),
            ((64, 384), BF),
            ((4, 64, 128), BF),
            ((9, 480, 128), BF),
            ((8, 64, 512), F32),
            ((19, 352, 128), BF),
        ],
        anywhere=[*range(1, 10), *range(13, 19)],
    )
    grad_one, grad_two, grad_three, grad_four = call(
        unpack_kernel,
        [((3, 3, 3, 4, 32), F32), ((864, 64), F32), ((27, 16, 128), F32), ((27, 32, 256), F32)],
        [summed(grads)],
        [((1152, 64), F32)],
    )
    grad_two = grad_two.reshape(3, 3, 3, 32, 64)
    grad_three = grad_three.reshape(3, 3, 3, 16, 128)
    grad_four = grad_four.reshape(3, 3, 3, 32, 256)
    return (features, grad_one, grad_two, grad_three, grad_four)


def solution(mesh):
    in_specs = (
        P(None, "space", "chan", None),
        P(),
        P(),
        P(None, None, None, "chan", None),
        P(None, None, None, "chan", None),
        P("chan", "space", None, None),
    )
    out_specs = (
        P("chan", "space", None, None),
        P(),
        P(),
        P(None, None, None, "chan", None),
        P(None, None, None, "chan", None),
    )
    return jax.shard_map(
        per_device, mesh=mesh, in_specs=in_specs, out_specs=out_specs, check_vma=False
    )
```

```python
import jax
import jax.numpy as jnp
import numpy as np
from jax import lax
from jax.experimental import pallas as pl
from jax.experimental.pallas import tpu as pltpu
from jax.sharding import PartitionSpec as P

BF = jnp.bfloat16
F32 = jnp.float32
BOTH = ("space", "chan")
LANES = 128
VMEM_LIMIT = 20 * 1024 * 1024


def mm(left, right):
    return lax.dot_general(left, right, (((1,), (0,)), ((), ())), preferred_element_type=F32)


def mm_nt(left, right):
    return lax.dot_general(left, right, (((1,), (1,)), ((), ())), preferred_element_type=F32)


def lane_of(shape):
    return lax.broadcasted_iota(jnp.int32, shape, len(shape) - 1)


def shifted(value, step):
    width = value.shape[1]
    turned = pltpu.roll(value, step % width, 1)
    edge = 0 if step == 1 else LANES - 1
    return jnp.where(lane_of(value.shape) % LANES == edge, 0.0, turned)


def activate(pre):
    sigma = jax.nn.sigmoid(pre)
    return pre * sigma, sigma * (1.0 + pre * (1.0 - sigma))


def call(kernel, outs, args, scratch=(), flops=0, anywhere=(), away=(), far=()):
    specs = []
    for place, a in enumerate(args):
        space = pltpu.SMEM if a.dtype == jnp.int32 else pltpu.VMEM
        specs.append(pl.BlockSpec(memory_space=pl.ANY if place in anywhere else space))
    size = sum(a.size * a.dtype.itemsize for a in args)
    args = [pltpu.with_memory_space_constraint(a, pltpu.HBM) if place in far else a for place, a in enumerate(args)]
    size += sum(int(np.prod(s)) * jnp.dtype(t).itemsize for s, t in outs)
    buffers = [pltpu.VMEM(s, t) for s, t in scratch]
    buffers.append(pltpu.SemaphoreType.DMA((28,)))
    places = [pltpu.HBM if place in away else pltpu.VMEM for place in range(len(outs))]
    return pl.pallas_call(
        kernel,
        out_shape=[
            pltpu.HBM(s, t) if place in away else jax.ShapeDtypeStruct(s, t)
            for place, (s, t) in enumerate(outs)
        ],
        in_specs=specs,
        out_specs=[pl.BlockSpec(memory_space=place) for place in places],
        scratch_shapes=buffers,
        compiler_params=pltpu.CompilerParams(vmem_limit_bytes=VMEM_LIMIT),
        cost_estimate=pl.CostEstimate(flops=flops, bytes_accessed=size, transcendentals=0),
    )(*args)


def begin(source, target, sem):
    copy = pltpu.make_async_copy(source, target, sem)
    copy.start()
    return copy


def picks(shape, column_of):
    row = lax.broadcasted_iota(jnp.int32, shape, 0)
    return jnp.where(column_of(row, lane_of(shape)), 1.0, 0.0).astype(BF)


def phase_matrix():
    return picks((512, 640), lambda row, lane: row == 4 * (lane % 128) + lane // 128)


def row_matrix():
    def at(row, lane):
        return lane == row // 4 % 8 * 64 + row % 4 * 16 + row // 32

    return picks((352, 320), at)


def first_layers_kernel(vol, w_one, w_two, *refs):
    field_out, act_one_out, slope_one_out, body, first, last, slope_two = refs[:7]
    field, act_one, slope_one, sems = refs[7:]
    phases = phase_matrix()
    rows = row_matrix()
    for start in range(0, 19, 4):
        planes = range(start, min(start + 4, 19))
        block = jnp.concatenate([jnp.reshape(vol[:, d], (64, 512)) for d in planes], 0)
        split = mm(block, phases).astype(BF)
        columns = []
        for n in range(len(planes)):
            parts = [split[n * 64 : n * 64 + 64, p * 128 : p * 128 + 128] for p in range(5)]
            columns.append(jnp.concatenate(parts, 0))
        placed = mm(rows, jnp.concatenate(columns, 1)).astype(BF)
        for n, d in enumerate(planes):
            field[d] = placed[:, n * 128 : n * 128 + 128]
    leaving = [begin(field, field_out, sems.at[0])]
    for d in range(9):
        columns = []
        for h in range(5):
            parts = [field[2 * d + a, h * 64 : h * 64 + 96] for a in range(3)]
            columns.append(jnp.concatenate(parts, 0))
        pre = mm(w_one[...], jnp.concatenate(columns, 1))
        act, slope = activate(pre)
        if d < 8:
            slope_one[d] = slope[:, :512]
        beside = shifted(act[:32], -1)
        for h in range(5):
            lanes = slice(h * 128, h * 128 + 128)
            act_one[d, h * 96 : h * 96 + 64] = act[:, lanes].astype(BF)
            act_one[d, h * 96 + 64 : h * 96 + 96] = beside[:, lanes].astype(BF)
    leaving.append(begin(slope_one, slope_one_out, sems.at[1]))
    leaving.append(begin(act_one, act_one_out, sems.at[2]))
    for d in range(4):
        columns = []
        for h in range(2):
            parts = [act_one[2 * d + a, h * 192 : h * 192 + 288] for a in range(3)]
            columns.append(jnp.concatenate(parts, 0))
        pre = mm(w_two[...], jnp.concatenate(columns, 1))
        act, slope = activate(pre)
        slope_two[d] = slope
        steep = slope.astype(BF)
        body[d, :, :256] = act.astype(BF)
        body[d, :, 256:] = steep[:, 128:]
        for rim, at in ((first, 0), (last, 3)):
            if d == at:
                rim[0, :, :256] = act.astype(BF)
                rim[0, :, 256:] = steep
    for copy in leaving:
        copy.wait()


def turned(me, blocks, count):
    wide = 4 * count
    row = lax.broadcasted_iota(jnp.int32, (count, wide), 0)
    pick = jnp.where(lane_of((count, wide)) == row + me * count, 1.0, 0.0).astype(BF)
    parts = []
    for c in range(3):
        rows = [blocks[j, ab * 3 + c] for ab in range(9) for j in range(4)]
        parts.append(mm_nt(pick, jnp.concatenate(rows, 0)).astype(BF))
    return jnp.concatenate(parts, 0)


def taps_of(field, d, start, width):
    parts = []
    for a in range(3):
        for b in range(3):
            parts.append(field[d + a, :, pl.ds(start + b * LANES, width)])
    return jnp.concatenate(parts, 0)


def shift_sum(product, channels):
    low = product[:channels]
    mid = product[channels : 2 * channels]
    high = product[2 * channels :]
    return shifted(low, 1) + mid + shifted(high, -1)


def clear_rims(field):
    depth, channels, lanes = field.shape
    rim = jnp.zeros((depth, channels, LANES), BF)
    field[:, :, :LANES] = rim
    field[:, :, lanes - LANES :] = rim


def arrive(refs, sems, target, up=1, width=1024):
    parts = len(refs) // 4 - 1
    copies = []
    for k in range(4):
        *bodies, rim = refs[k * (parts + 1) : (k + 1) * (parts + 1)]
        lanes = pl.ds(0, width)
        planes = 4 // parts
        pieces = [(body.at[:, :, lanes], up + n * planes, planes) for n, body in enumerate(bodies)]
        pieces.append((rim.at[pl.ds(0, up), :, lanes], 0, up))
        pieces.append((rim.at[pl.ds(up, 1), :, lanes], up + 4, 1))
        for n, (source, first, count) in enumerate(pieces):
            copies.append(pltpu.make_async_copy(source, target(k, first, count), sems.at[4 * k + n]))
    for copy in copies:
        copy.start()
    return copies


def assemble(field, me, refs, sems, channels, up=1, rim=1):
    def target(k, first, count):
        at = pl.multiple_of((me ^ k) * channels, channels)
        return field.at[pl.ds(first, count), pl.ds(at, channels), pl.ds(rim * LANES, 8 * LANES)]

    return arrive(refs, sems, target, up)


def turn_kernel(me_ref, filters, weights, kernel, sems):
    arrived = begin(filters.at[:, :, pl.ds(32, 16), pl.ds(0, LANES)], kernel, sems.at[0])
    arrived.wait()
    weights[...] = turned(me_ref[0], kernel, 32)


def third_kernel(me_ref, *refs):
    blocks, weights = refs[:8], refs[8]
    act, first, last, slope_out, own_out, front_out, row_out = refs[9:16]
    field, slope, front, row, sems = refs[16:]
    me = me_ref[0]

    def target(k, first, count):
        at = pl.multiple_of(LANES + (me ^ k) * (2 * LANES), LANES)
        return field.at[pl.ds(first, count), :, pl.ds(at, 2 * LANES)]

    copies = arrive(blocks, sems, target, 1, 2 * LANES)
    plane = begin(blocks[1].at[0, :, pl.ds(256, 256)], front.at[:, pl.ds(LANES, 256)], sems.at[21])

    @pl.when(me == 0)
    def _():
        front[:, :LANES] = jnp.zeros((64, LANES), BF)
        row[...] = jnp.zeros((4, 64, LANES), BF)

    for k in (1, 3):

        @pl.when((me > 0) & (me ^ k == me - 1))
        def _(k=k):
            begin(blocks[2 * k + 1].at[0, :, pl.ds(384, LANES)], front.at[:, pl.ds(0, LANES)], sems.at[22])
            begin(blocks[2 * k].at[:, :, pl.ds(256, LANES)], row, sems.at[23])

    clear_rims(field)
    plane.wait()

    @pl.when(me > 0)
    def _():
        corner = blocks[1].at[0, :, pl.ds(384, LANES)]
        pltpu.make_async_copy(corner, front.at[:, pl.ds(0, LANES)], sems.at[22]).wait()
        pltpu.make_async_copy(blocks[0].at[:, :, pl.ds(256, LANES)], row, sems.at[23]).wait()

    leaving = [begin(front, front_out, sems.at[24]), begin(row, row_out, sems.at[25])]
    for copy in copies:
        copy.wait()
    own = field.at[:, pl.ds(pl.multiple_of(me * 16, 16), 16), :]
    leaving.append(begin(own, own_out, sems.at[26]))
    for d in range(4):
        product = mm(weights[...], taps_of(field, d, 0, 1024))
        value, steep = activate(shift_sum(product, 32))
        act[d] = value.astype(BF)
        slope[d] = steep
    first[0] = act[0]
    last[0] = act[3]
    leaving.append(begin(slope, slope_out, sems.at[27]))
    for copy in leaving:
        copy.wait()


def fourth_kernel(me_ref, *refs):
    blocks, filters, cotangent = refs[:8], refs[8], refs[9]
    features, back, first, last, field, kernel, sems = refs[10:]
    me = me_ref[0]
    arrived = begin(filters.at[:, :, pl.ds(0, 32), :], kernel, sems.at[20])
    copies = assemble(field, me, blocks, sems, 32)
    clear_rims(field)
    arrived.wait()
    weights = turned(me, kernel, 64)
    for copy in copies:
        copy.wait()
    for d in range(4):
        product = mm(weights, taps_of(field, d, 0, 1024))
        value, steep = activate(shift_sum(product, 64))
        features[d] = value.astype(BF)
        back[d] = (cotangent[d].astype(F32) * steep).astype(BF)
    first[0] = back[0]
    last[0] = back[3]


def flipped_weights(kernel):
    columns = []
    for a in range(3):
        for b in range(3):
            taps = [((2 - a) * 3 + 2 - b) * 3 + 2 - c for c in range(3)]
            columns.append(jnp.concatenate([kernel[t] for t in taps], 0))
    return jnp.concatenate(columns, 1)


def into_three_kernel(me_ref, *refs):
    blocks, kernel, steep = refs[:8], refs[8], refs[9]
    back, first, last, field, slope, sems = refs[10:]
    copies = assemble(field, me_ref[0], blocks, sems, 64)
    copies.append(begin(steep, slope, sems.at[20]))
    clear_rims(field)
    weights = flipped_weights(kernel)
    for copy in copies:
        copy.wait()
    for d in range(4):
        product = mm(weights, taps_of(field, d, 0, 1024))
        back[d] = (shift_sum(product, 32) * slope[d]).astype(BF)
    first[0] = back[0]
    last[...] = back[2:]


def three_shifts(value):
    wide = value.astype(F32)
    return jnp.concatenate([shifted(wide, 1).astype(BF), value, shifted(wide, -1).astype(BF)], 0)


def filter_grad(wide, gradients):
    total = None
    for d in range(4):
        term = mm_nt(taps_of(wide, d, 0, 1024), gradients(d))
        total = term if total is None else total + term
    return total


def grad_four_kernel(me_ref, own, rim, *refs):
    blocks, grad, wide, gradient, sems = refs[:4], *refs[4:]
    copies = []
    for k in range(4):
        at = pl.multiple_of((me_ref[0] ^ k) * 64, 64)
        copies.append(begin(blocks[k], gradient.at[:, pl.ds(at, 64), :], sems.at[k]))
    clear_rims(wide)
    inside = slice(LANES, 9 * LANES)
    wide[0, :, inside] = three_shifts(rim[0])
    for d in range(4):
        wide[d + 1, :, inside] = three_shifts(own[d])
    wide[5, :, inside] = three_shifts(rim[1])
    for copy in copies:
        copy.wait()
    grad[...] = filter_grad(wide, lambda d: gradient[d]).astype(BF)


def last_kernel(me_ref, *refs):
    blocks = refs[:8]
    filters, w_back, act_two, grad_four = refs[8:12]
    away, out, field, shifts, wide, back_one, kernel = refs[12:18], *refs[18:24]
    slope, front, row, act_one, slope_one, volume = refs[24:30]
    sems = refs[30]
    me = me_ref[0]
    arrived = begin(filters.at[:, :, pl.ds(32, 16), pl.ds(0, LANES)], kernel, sems.at[20])
    copies = assemble(field, me, blocks, sems, 32, up=2, rim=2)
    later = [begin(source, refs[24 + n], sems.at[21 + n]) for n, source in enumerate(away)]
    field[:, :, : 2 * LANES] = jnp.zeros((7, 128, 2 * LANES), BF)
    field[:, :, 10 * LANES :] = jnp.zeros((7, 128, LANES), BF)
    clear_rims(shifts)
    inside = slice(LANES, 9 * LANES)
    for d in range(6):
        shifts[d, :, inside] = three_shifts(act_two[d, :, inside])
    for t in range(27):
        out[t, :32] = grad_four[t]
    for t in range(27, 32):
        out[t] = jnp.zeros((48, 256), BF)
    arrived.wait()
    taps = [jnp.concatenate([kernel[j, t] for j in range(4)], 0) for t in range(27)]
    weights = flipped_weights(taps)
    for copy in copies + later:
        copy.wait()

    start = pl.multiple_of(me * (2 * LANES), LANES)
    for d in range(5):
        steep = front[...].astype(F32)
        if d > 0:
            steep = jnp.concatenate([row[d - 1].astype(F32), slope[d - 1]], 1)
        product = mm(weights, taps_of(field, d, start, 3 * LANES))
        value = shift_sum(product, 64) * steep
        value = value.astype(BF)
        beside = shifted(value.astype(F32), 1).astype(BF)
        for h in range(3):
            wide[d, h, :64] = value[:, h * 128 : h * 128 + 128]
            wide[d, h, 64:] = beside[:, h * 128 : h * 128 + 128]
    for d_odd in range(2):
        for h_odd in range(2):
            taps = [(a, b) for a in ((1,) if d_odd else (0, 2)) for b in ((1,) if h_odd else (0, 2))]
            mixed = jnp.concatenate([w_back[a * 3 + b] for a, b in taps], 1)
            columns = []
            for d in range(4):
                for h in range(2):
                    parts = [wide[d + 1 - a // 2, h + 1 - b // 2] for a, b in taps]
                    columns.append(jnp.concatenate(parts, 0))
            into = mm(mixed, jnp.concatenate(columns, 1))
            for d in range(4):
                for h in range(2):
                    at = (d * 2 + h) * 128
                    lanes = slice((2 * h + h_odd) * 128, (2 * h + h_odd) * 128 + 128)
                    d_one = 2 * d + d_odd
                    value = into[:, at : at + 128] * slope_one[d_one, :, lanes]
                    back_one[d_one, :, lanes] = value.astype(BF)
    three = filter_grad(shifts, lambda d: field[d + 2, :, 2 * LANES : 10 * LANES]).astype(BF)
    for t in range(27):
        out[t, 32:, :128] = three[t * 16 : t * 16 + 16]
    two = None
    for d in range(4):
        columns = []
        for h in range(2):
            parts = [act_one[2 * d + a, h * 192 : h * 192 + 288] for a in range(3)]
            columns.append(jnp.concatenate(parts, 0))
        own = jnp.concatenate([wide[d + 1, 1, :64], wide[d + 1, 2, :64]], 1)
        term = mm_nt(jnp.concatenate(columns, 1), own)
        two = term if two is None else two + term
    one = None
    for d in range(8):
        columns = []
        for h in range(4):
            parts = [volume[2 * d + a, h * 64 : h * 64 + 96] for a in range(3)]
            columns.append(jnp.concatenate(parts, 0))
        term = mm_nt(jnp.concatenate(columns, 1), back_one[d])
        one = term if one is None else one + term
    both = jnp.concatenate([two, one], 0)
    for t in range(32):
        pair = [both[32 * t + 16 * q : 32 * t + 16 * q + 16] for q in range(2)]
        out[t, 32:, 128:] = jnp.concatenate(pair, 1).astype(BF)
    rest = [both[1024 + 32 * q : 1056 + 32 * q] for q in range(4)]
    out[27, :32] = jnp.concatenate(rest, 1).astype(BF)


def unpack_kernel(packed, grad_one, grad_two, grad_three, grad_four, both, sems):
    for t in range(27):
        grad_four[t] = packed[t, :32].astype(F32)
        grad_three[t] = packed[t, 32:, :128].astype(F32)
    for t in range(32):
        pair = packed[t, 32:, 128:].astype(F32)
        both[32 * t : 32 * t + 16] = pair[:, :64]
        both[32 * t + 16 : 32 * t + 32] = pair[:, 64:]
    rest = packed[27, :32].astype(F32)
    for q in range(4):
        both[1024 + 32 * q : 1056 + 32 * q] = rest[:, 64 * q : 64 * q + 64]
    grad_two[...] = both[:864]
    for t in range(9):
        at = 864 + 32 * t
        value = both[at : at + 12, :32] + both[at + 8 : at + 20, 32:]
        for c in range(3):
            grad_one[t // 3, t % 3, c] = value[4 * c : 4 * c + 4]


def moved(block, depth_step, chan_of):
    depth, chans = lax.axis_size("space"), lax.axis_size("chan")
    route = []
    for s in range(depth):
        for c in range(chans):
            to = chan_of(c)
            if 0 <= s + depth_step < depth and 0 <= to < chans:
                route.append((s * chans + c, (s + depth_step) * chans + to))
    return lax.ppermute(block, BOTH, route)


def gathered(own, first, last, meanwhile=None):
    across = [moved(part, 0, lambda c: c ^ 2) for part in own]
    up = moved(last, 1, lambda c: c)
    down = moved(first, -1, lambda c: c)
    core = [moved(part, 0, lambda c: c ^ 1) for part in own]
    rim = jnp.concatenate([up, down], 0)
    across_rim = moved(rim, 0, lambda c: c ^ 2)
    across, held, meanwhile = lax.optimization_barrier((across, rim, meanwhile))
    core_rim = moved(held, 0, lambda c: c ^ 1)
    pair = [moved(piece, 0, lambda c: c ^ 1) for piece in (*across, across_rim)]
    blocks = [*own, rim, *core, core_rim, *across, across_rim, *pair]
    return blocks if meanwhile is None else (blocks, meanwhile)


def summed(parts):
    terms = lax.all_to_all(parts, "space", 0, 0)
    own = jnp.sum(terms.astype(F32), 0)
    shape = own.shape
    row = lax.broadcasted_iota(jnp.int32, shape, 0)
    shared = (row >= 32) & (lane_of(shape) >= 128) | (lax.axis_index("space") == 27)
    both = own
    for step in (1, 2):
        sent = lax.optimization_barrier(both.astype(BF))
        both = sent.astype(F32) + moved(sent, 0, lambda c, step=step: c ^ step).astype(F32)
    total = jnp.where(shared, both, own).astype(BF)
    return lax.all_to_all(jnp.broadcast_to(total[None], parts.shape), "space", 0, 0)


def per_device(volume, kernel_one, kernel_two, kernel_three, kernel_four, cotangent):
    me = lax.axis_index("chan").astype(jnp.int32)[None]
    below = moved(volume[:, :3], -1, lambda c: c)
    beside = moved(volume[:, :, :3], 0, lambda c: c - 1)
    corner = moved(volume[:, :3, :3], -1, lambda c: c - 1)

    three = jnp.pad(kernel_three.reshape(27, 16, 128), ((0, 0), (0, 0), (0, 128)))
    four = kernel_four.reshape(27, 32, 256)
    filters = lax.all_gather(jnp.concatenate([four, three], 1), "chan")
    cotangent = jnp.transpose(cotangent.reshape(64, 4, 1024), (1, 0, 2))
    corner, cotangent = lax.optimization_barrier((corner, cotangent))

    even = jnp.pad(kernel_one, ((0, 0), (0, 0), (0, 5), (0, 0), (0, 0)))
    odd = jnp.pad(kernel_one, ((0, 0), (0, 0), (2, 3), (0, 0), (0, 0)))
    w_one = jnp.stack([even, odd]).reshape(2, 288, 32).transpose(0, 2, 1).reshape(64, 288)
    w_two = kernel_two.reshape(864, 64).T
    top = jnp.concatenate([kernel_two[:, :, 0], kernel_two[:, :, 2]], 3)
    bottom = jnp.pad(kernel_two[:, :, 1], ((0, 0), (0, 0), (0, 0), (0, 64)))
    w_back = jnp.concatenate([top, bottom], 2).reshape(9, 64, 128)

    tall = jnp.concatenate([volume, below], 1)
    side = jnp.pad(jnp.concatenate([beside, corner], 1), ((0, 0), (0, 0), (0, 5), (0, 0)))
    tall = jnp.concatenate([tall, side], 2)

    field, act_one, slope_one, body, first, last, slope_two = call(
        first_layers_kernel,
        [
            ((19, 352, 128), BF),
            ((9, 480, 128), BF),
            ((8, 64, 512), F32),
            ((4, 64, 384), BF),
            ((1, 64, 512), BF),
            ((1, 64, 512), BF),
            ((4, 64, 256), F32),
        ],
        [tall, w_one, w_two],
        [((19, 352, 128), BF), ((9, 480, 128), BF), ((8, 64, 512), F32)],
        away=(0, 1, 2),
    )
    pieces = range(1, 9)
    (w_three,) = call(
        turn_kernel, [((96, 576), BF)], [me, filters], [((4, 27, 16, 128), BF)], anywhere=(1,), far=(1,)
    )
    blocks, w_three = gathered([body], first, last, w_three)
    act_three, first, last, slope_three, own_two, front, row = call(
        third_kernel,
        [((4, 32, 1024), BF), ((1, 32, 1024), BF), ((1, 32, 1024), BF), ((4, 32, 1024), F32), ((6, 16, 1280), BF), ((64, 384), BF), ((4, 64, 128), BF)],
        [me, *blocks, w_three],
        [((6, 64, 1280), BF), ((4, 32, 1024), F32), ((64, 384), BF), ((4, 64, 128), BF)],
        anywhere=pieces,
        away=(3, 4, 5, 6),
    )
    blocks = gathered([act_three], first, last)
    features, back_four, first, last = call(
        fourth_kernel,
        [((4, 64, 1024), BF), ((4, 64, 1024), BF), ((1, 64, 1024), BF), ((1, 64, 1024), BF)],
        [me, *blocks, filters, cotangent],
        [((6, 128, 1280), BF), ((4, 27, 32, 256), BF)],
        anywhere=range(1, 10),
    )
    features = jnp.transpose(features, (1, 0, 2)).reshape(64, 4, 8, 128)
    all_four = gathered([back_four], first, last)
    back_three, first, last = call(
        into_three_kernel,
        [((4, 32, 1024), BF), ((1, 32, 1024), BF), ((2, 32, 1024), BF)],
        [me, *all_four, four, slope_three],
        [((6, 256, 1280), BF), ((4, 32, 1024), F32)],
        anywhere=[*range(1, 9), 10],
    )
    (grad_four,) = call(
        grad_four_kernel,
        [((864, 256), BF)],
        [me, *blocks[:2], *all_four[::2]],
        [((6, 96, 1280), BF), ((4, 256, 1024), BF)],
        flops=2 * 864 * 256 * 4096,
        anywhere=range(3, 7),
    )
    blocks, grad_four = gathered([back_three], first, last, grad_four)
    (grads,) = call(
        last_kernel,
        [((32, 48, 256), BF)],
        [
            me,
            *blocks,
            filters,
            w_back,
            own_two,
            grad_four.reshape(27, 32, 256),
            slope_two,
            front,
            row,
            act_one,
            slope_one,
            field,
        ],
        [
            ((7, 128, 1408), BF),
            ((6, 48, 1280), BF),
            ((5, 3, 128, 128), BF),
            ((8, 64, 512), BF),
            ((4, 27, 16, 128), BF),
            ((4, 64, 256), F32),
            ((64, 384), BF),
            ((4, 64, 128), BF),
            ((9, 480, 128), BF),
            ((8, 64, 512), F32),
            ((19, 352, 128), BF),
        ],
        anywhere=[*range(1, 10), *range(13, 19)],
    )
    grad_one, grad_two, grad_three, grad_four = call(
        unpack_kernel,
        [((3, 3, 3, 4, 32), F32), ((864, 64), F32), ((27, 16, 128), F32), ((27, 32, 256), F32)],
        [summed(grads)],
        [((1152, 64), F32)],
    )
    grad_two = grad_two.reshape(3, 3, 3, 32, 64)
    grad_three = grad_three.reshape(3, 3, 3, 16, 128)
    grad_four = grad_four.reshape(3, 3, 3, 32, 256)
    return (features, grad_one, grad_two, grad_three, grad_four)


def solution(mesh):
    in_specs = (
        P(None, "space", "chan", None),
        P(),
        P(),
        P(None, None, None, "chan", None),
        P(None, None, None, "chan", None),
        P("chan", "space", None, None),
    )
    out_specs = (
        P("chan", "space", None, None),
        P(),
        P(),
        P(None, None, None, "chan", None),
        P(None, None, None, "chan", None),
    )
    return jax.shard_map(
        per_device, mesh=mesh, in_specs=in_specs, out_specs=out_specs, check_vma=False
    )
```

```python
import jax
import jax.numpy as jnp
import numpy as np
from jax import lax
from jax.experimental import pallas as pl
from jax.experimental.pallas import tpu as pltpu
from jax.sharding import PartitionSpec as P

BF = jnp.bfloat16
F32 = jnp.float32
BOTH = ("space", "chan")
LANES = 128
VMEM_LIMIT = 20 * 1024 * 1024


def mm(left, right):
    return lax.dot_general(left, right, (((1,), (0,)), ((), ())), preferred_element_type=F32)


def mm_nt(left, right):
    return lax.dot_general(left, right, (((1,), (1,)), ((), ())), preferred_element_type=F32)


def lane_of(shape):
    return lax.broadcasted_iota(jnp.int32, shape, len(shape) - 1)


def shifted(value, step):
    width = value.shape[1]
    turned = pltpu.roll(value, step % width, 1)
    edge = 0 if step == 1 else LANES - 1
    return jnp.where(lane_of(value.shape) % LANES == edge, 0.0, turned)


def activate(pre):
    sigma = jax.nn.sigmoid(pre)
    return pre * sigma, sigma * (1.0 + pre * (1.0 - sigma))


def call(kernel, outs, args, scratch=(), flops=0, anywhere=(), away=(), far=()):
    specs = []
    for place, a in enumerate(args):
        space = pltpu.SMEM if a.dtype == jnp.int32 else pltpu.VMEM
        specs.append(pl.BlockSpec(memory_space=pl.ANY if place in anywhere else space))
    size = sum(a.size * a.dtype.itemsize for a in args)
    args = [pltpu.with_memory_space_constraint(a, pltpu.HBM) if place in far else a for place, a in enumerate(args)]
    size += sum(int(np.prod(s)) * jnp.dtype(t).itemsize for s, t in outs)
    buffers = [pltpu.VMEM(s, t) for s, t in scratch]
    buffers.append(pltpu.SemaphoreType.DMA((28,)))
    places = [pltpu.HBM if place in away else pltpu.VMEM for place in range(len(outs))]
    return pl.pallas_call(
        kernel,
        out_shape=[
            pltpu.HBM(s, t) if place in away else jax.ShapeDtypeStruct(s, t)
            for place, (s, t) in enumerate(outs)
        ],
        in_specs=specs,
        out_specs=[pl.BlockSpec(memory_space=place) for place in places],
        scratch_shapes=buffers,
        compiler_params=pltpu.CompilerParams(vmem_limit_bytes=VMEM_LIMIT),
        cost_estimate=pl.CostEstimate(flops=flops, bytes_accessed=size, transcendentals=0),
    )(*args)


def begin(source, target, sem):
    copy = pltpu.make_async_copy(source, target, sem)
    copy.start()
    return copy


def picks(shape, column_of):
    row = lax.broadcasted_iota(jnp.int32, shape, 0)
    return jnp.where(column_of(row, lane_of(shape)), 1.0, 0.0).astype(BF)


def phase_matrix():
    return picks((512, 640), lambda row, lane: row == 4 * (lane % 128) + lane // 128)


def row_matrix():
    def at(row, lane):
        return lane == row // 4 % 8 * 64 + row % 4 * 16 + row // 32

    return picks((352, 320), at)


def first_layers_kernel(vol, w_one, w_two, *refs):
    field_out, act_one_out, slope_one_out, body, first, last, slope_two = refs[:7]
    field, act_one, slope_one, sems = refs[7:]
    phases = phase_matrix()
    rows = row_matrix()
    for start in range(0, 19, 4):
        planes = range(start, min(start + 4, 19))
        block = jnp.concatenate([jnp.reshape(vol[:, d], (64, 512)) for d in planes], 0)
        split = mm(block, phases).astype(BF)
        columns = []
        for n in range(len(planes)):
            parts = [split[n * 64 : n * 64 + 64, p * 128 : p * 128 + 128] for p in range(5)]
            columns.append(jnp.concatenate(parts, 0))
        placed = mm(rows, jnp.concatenate(columns, 1)).astype(BF)
        for n, d in enumerate(planes):
            field[d] = placed[:, n * 128 : n * 128 + 128]
    leaving = [begin(field, field_out, sems.at[0])]
    for d in range(9):
        columns = []
        for h in range(5):
            parts = [field[2 * d + a, h * 64 : h * 64 + 96] for a in range(3)]
            columns.append(jnp.concatenate(parts, 0))
        pre = mm(w_one[...], jnp.concatenate(columns, 1))
        act, slope = activate(pre)
        if d < 8:
            slope_one[d] = slope[:, :512]
        beside = shifted(act[:32], -1)
        for h in range(5):
            lanes = slice(h * 128, h * 128 + 128)
            act_one[d, h * 96 : h * 96 + 64] = act[:, lanes].astype(BF)
            act_one[d, h * 96 + 64 : h * 96 + 96] = beside[:, lanes].astype(BF)
    leaving.append(begin(slope_one, slope_one_out, sems.at[1]))
    leaving.append(begin(act_one, act_one_out, sems.at[2]))
    for d in range(4):
        columns = []
        for h in range(2):
            parts = [act_one[2 * d + a, h * 192 : h * 192 + 288] for a in range(3)]
            columns.append(jnp.concatenate(parts, 0))
        pre = mm(w_two[...], jnp.concatenate(columns, 1))
        act, slope = activate(pre)
        slope_two[d] = slope
        steep = slope.astype(BF)
        body[d, :, :256] = act.astype(BF)
        body[d, :, 256:] = steep[:, 128:]
        for rim, at in ((first, 0), (last, 3)):
            if d == at:
                rim[0, :, :256] = act.astype(BF)
                rim[0, :, 256:] = steep
    for copy in leaving:
        copy.wait()


def turned(me, blocks, count):
    wide = 4 * count
    row = lax.broadcasted_iota(jnp.int32, (count, wide), 0)
    pick = jnp.where(lane_of((count, wide)) == row + me * count, 1.0, 0.0).astype(BF)
    parts = []
    for c in range(3):
        rows = [blocks[j, ab * 3 + c] for ab in range(9) for j in range(4)]
        parts.append(mm_nt(pick, jnp.concatenate(rows, 0)).astype(BF))
    return jnp.concatenate(parts, 0)


def taps_of(field, d, start, width):
    parts = []
    for a in range(3):
        for b in range(3):
            parts.append(field[d + a, :, pl.ds(start + b * LANES, width)])
    return jnp.concatenate(parts, 0)


def shift_sum(product, channels):
    low = product[:channels]
    mid = product[channels : 2 * channels]
    high = product[2 * channels :]
    return shifted(low, 1) + mid + shifted(high, -1)


def clear_rims(field):
    depth, channels, lanes = field.shape
    rim = jnp.zeros((depth, channels, LANES), BF)
    field[:, :, :LANES] = rim
    field[:, :, lanes - LANES :] = rim


def arrive(refs, sems, target, up=1, width=1024):
    parts = len(refs) // 4 - 1
    copies = []
    for k in range(4):
        *bodies, rim = refs[k * (parts + 1) : (k + 1) * (parts + 1)]
        lanes = pl.ds(0, width)
        planes = 4 // parts
        pieces = [(body.at[:, :, lanes], up + n * planes, planes) for n, body in enumerate(bodies)]
        pieces.append((rim.at[pl.ds(0, up), :, lanes], 0, up))
        pieces.append((rim.at[pl.ds(up, 1), :, lanes], up + 4, 1))
        for n, (source, first, count) in enumerate(pieces):
            copies.append(pltpu.make_async_copy(source, target(k, first, count), sems.at[4 * k + n]))
    for copy in copies:
        copy.start()
    return copies


def assemble(field, me, refs, sems, channels, up=1, rim=1):
    def target(k, first, count):
        at = pl.multiple_of((me ^ k) * channels, channels)
        return field.at[pl.ds(first, count), pl.ds(at, channels), pl.ds(rim * LANES, 8 * LANES)]

    return arrive(refs, sems, target, up)


def turn_kernel(me_ref, filters, weights, kernel, sems):
    arrived = begin(filters.at[:, :, pl.ds(32, 16), pl.ds(0, LANES)], kernel, sems.at[0])
    arrived.wait()
    weights[...] = turned(me_ref[0], kernel, 32)


def third_kernel(me_ref, *refs):
    blocks, weights = refs[:8], refs[8]
    act, first, last, slope_out, own_out, front_out, row_out = refs[9:16]
    field, slope, front, row, sems = refs[16:]
    me = me_ref[0]

    def target(k, first, count):
        at = pl.multiple_of(LANES + (me ^ k) * (2 * LANES), LANES)
        return field.at[pl.ds(first, count), :, pl.ds(at, 2 * LANES)]

    copies = arrive(blocks, sems, target, 1, 2 * LANES)
    plane = begin(blocks[1].at[0, :, pl.ds(256, 256)], front.at[:, pl.ds(LANES, 256)], sems.at[21])

    @pl.when(me == 0)
    def _():
        front[:, :LANES] = jnp.zeros((64, LANES), BF)
        row[...] = jnp.zeros((4, 64, LANES), BF)

    for k in (1, 3):

        @pl.when((me > 0) & (me ^ k == me - 1))
        def _(k=k):
            begin(blocks[2 * k + 1].at[0, :, pl.ds(384, LANES)], front.at[:, pl.ds(0, LANES)], sems.at[22])
            begin(blocks[2 * k].at[:, :, pl.ds(256, LANES)], row, sems.at[23])

    clear_rims(field)
    plane.wait()

    @pl.when(me > 0)
    def _():
        corner = blocks[1].at[0, :, pl.ds(384, LANES)]
        pltpu.make_async_copy(corner, front.at[:, pl.ds(0, LANES)], sems.at[22]).wait()
        pltpu.make_async_copy(blocks[0].at[:, :, pl.ds(256, LANES)], row, sems.at[23]).wait()

    leaving = [begin(front, front_out, sems.at[24]), begin(row, row_out, sems.at[25])]
    for copy in copies:
        copy.wait()
    own = field.at[:, pl.ds(pl.multiple_of(me * 16, 16), 16), :]
    leaving.append(begin(own, own_out, sems.at[26]))
    for d in range(4):
        product = mm(weights[...], taps_of(field, d, 0, 1024))
        value, steep = activate(shift_sum(product, 32))
        act[d] = value.astype(BF)
        slope[d] = steep
    first[0] = act[0]
    last[0] = act[3]
    leaving.append(begin(slope, slope_out, sems.at[27]))
    for copy in leaving:
        copy.wait()


def fourth_kernel(me_ref, *refs):
    blocks, filters, cotangent = refs[:8], refs[8], refs[9]
    features, back, first, last, field, sems = refs[10:]
    me = me_ref[0]
    copies = assemble(field, me, blocks, sems, 32)
    clear_rims(field)
    weights = turned(me, filters.at[:, :, :32], 64)
    for copy in copies:
        copy.wait()
    for d in range(4):
        product = mm(weights, taps_of(field, d, 0, 1024))
        value, steep = activate(shift_sum(product, 64))
        features[d] = value.astype(BF)
        back[d] = (cotangent[d].astype(F32) * steep).astype(BF)
    first[0] = back[0]
    last[0] = back[3]


def flipped_weights(kernel):
    columns = []
    for a in range(3):
        for b in range(3):
            taps = [((2 - a) * 3 + 2 - b) * 3 + 2 - c for c in range(3)]
            columns.append(jnp.concatenate([kernel[t] for t in taps], 0))
    return jnp.concatenate(columns, 1)


def into_three_kernel(me_ref, *refs):
    blocks, kernel, slope = refs[:8], refs[8], refs[9]
    back, first, last, field, sems = refs[10:]
    copies = assemble(field, me_ref[0], blocks, sems, 64)
    clear_rims(field)
    weights = flipped_weights(kernel)
    for copy in copies:
        copy.wait()
    for d in range(4):
        product = mm(weights, taps_of(field, d, 0, 1024))
        back[d] = (shift_sum(product, 32) * slope[d]).astype(BF)
    first[0] = back[0]
    last[...] = back[2:]


def three_shifts(value):
    wide = value.astype(F32)
    return jnp.concatenate([shifted(wide, 1).astype(BF), value, shifted(wide, -1).astype(BF)], 0)


def filter_grad(wide, gradients):
    total = None
    for d in range(4):
        term = mm_nt(taps_of(wide, d, 0, 1024), gradients(d))
        total = term if total is None else total + term
    return total


def grad_four_kernel(me_ref, own, rim, *refs):
    blocks, grad, wide, gradient, sems = refs[:4], *refs[4:]
    copies = []
    for k in range(4):
        at = pl.multiple_of((me_ref[0] ^ k) * 64, 64)
        copies.append(begin(blocks[k], gradient.at[:, pl.ds(at, 64), :], sems.at[k]))
    clear_rims(wide)
    inside = slice(LANES, 9 * LANES)
    wide[0, :, inside] = three_shifts(rim[0])
    for d in range(4):
        wide[d + 1, :, inside] = three_shifts(own[d])
    wide[5, :, inside] = three_shifts(rim[1])
    for copy in copies:
        copy.wait()
    grad[...] = filter_grad(wide, lambda d: gradient[d]).astype(BF)


def last_kernel(me_ref, *refs):
    blocks = refs[:8]
    filters, w_back, act_two, grad_four = refs[8:12]
    slope, front, row, act_one, slope_one, volume = refs[12:18]
    out, field, shifts, wide, back_one, sems = refs[18:]
    me = me_ref[0]
    copies = assemble(field, me, blocks, sems, 32, up=2, rim=2)
    field[:, :, : 2 * LANES] = jnp.zeros((7, 128, 2 * LANES), BF)
    field[:, :, 10 * LANES :] = jnp.zeros((7, 128, LANES), BF)
    clear_rims(shifts)
    inside = slice(LANES, 9 * LANES)
    for d in range(6):
        shifts[d, :, inside] = three_shifts(act_two[d, :, inside])
    for t in range(27):
        out[t, :32] = grad_four[t]
    for t in range(27, 32):
        out[t] = jnp.zeros((48, 256), BF)
    taps = [jnp.concatenate([filters[j, t, 32:, :LANES] for j in range(4)], 0) for t in range(27)]
    weights = flipped_weights(taps)
    for copy in copies:
        copy.wait()

    start = pl.multiple_of(me * (2 * LANES), LANES)
    for d in range(5):
        steep = front[...].astype(F32)
        if d > 0:
            steep = jnp.concatenate([row[d - 1].astype(F32), slope[d - 1]], 1)
        product = mm(weights, taps_of(field, d, start, 3 * LANES))
        value = shift_sum(product, 64) * steep
        value = value.astype(BF)
        beside = shifted(value.astype(F32), 1).astype(BF)
        for h in range(3):
            wide[d, h, :64] = value[:, h * 128 : h * 128 + 128]
            wide[d, h, 64:] = beside[:, h * 128 : h * 128 + 128]
    for d_odd in range(2):
        for h_odd in range(2):
            taps = [(a, b) for a in ((1,) if d_odd else (0, 2)) for b in ((1,) if h_odd else (0, 2))]
            mixed = jnp.concatenate([w_back[a * 3 + b] for a, b in taps], 1)
            columns = []
            for d in range(4):
                for h in range(2):
                    parts = [wide[d + 1 - a // 2, h + 1 - b // 2] for a, b in taps]
                    columns.append(jnp.concatenate(parts, 0))
            into = mm(mixed, jnp.concatenate(columns, 1))
            for d in range(4):
                for h in range(2):
                    at = (d * 2 + h) * 128
                    lanes = slice((2 * h + h_odd) * 128, (2 * h + h_odd) * 128 + 128)
                    d_one = 2 * d + d_odd
                    value = into[:, at : at + 128] * slope_one[d_one, :, lanes]
                    back_one[d_one, :, lanes] = value.astype(BF)
    three = filter_grad(shifts, lambda d: field[d + 2, :, 2 * LANES : 10 * LANES]).astype(BF)
    for t in range(27):
        out[t, 32:, :128] = three[t * 16 : t * 16 + 16]
    two = None
    for d in range(4):
        columns = []
        for h in range(2):
            parts = [act_one[2 * d + a, h * 192 : h * 192 + 288] for a in range(3)]
            columns.append(jnp.concatenate(parts, 0))
        own = jnp.concatenate([wide[d + 1, 1, :64], wide[d + 1, 2, :64]], 1)
        term = mm_nt(jnp.concatenate(columns, 1), own)
        two = term if two is None else two + term
    one = None
    for d in range(8):
        columns = []
        for h in range(4):
            parts = [volume[2 * d + a, h * 64 : h * 64 + 96] for a in range(3)]
            columns.append(jnp.concatenate(parts, 0))
        term = mm_nt(jnp.concatenate(columns, 1), back_one[d])
        one = term if one is None else one + term
    both = jnp.concatenate([two, one], 0)
    for t in range(32):
        pair = [both[32 * t + 16 * q : 32 * t + 16 * q + 16] for q in range(2)]
        out[t, 32:, 128:] = jnp.concatenate(pair, 1).astype(BF)
    rest = [both[1024 + 32 * q : 1056 + 32 * q] for q in range(4)]
    out[27, :32] = jnp.concatenate(rest, 1).astype(BF)


def unpack_kernel(packed, grad_one, grad_two, grad_three, grad_four, both, sems):
    for t in range(27):
        grad_four[t] = packed[t, :32].astype(F32)
        grad_three[t] = packed[t, 32:, :128].astype(F32)
    for t in range(32):
        pair = packed[t, 32:, 128:].astype(F32)
        both[32 * t : 32 * t + 16] = pair[:, :64]
        both[32 * t + 16 : 32 * t + 32] = pair[:, 64:]
    rest = packed[27, :32].astype(F32)
    for q in range(4):
        both[1024 + 32 * q : 1056 + 32 * q] = rest[:, 64 * q : 64 * q + 64]
    grad_two[...] = both[:864]
    for t in range(9):
        at = 864 + 32 * t
        value = both[at : at + 12, :32] + both[at + 8 : at + 20, 32:]
        for c in range(3):
            grad_one[t // 3, t % 3, c] = value[4 * c : 4 * c + 4]


def moved(block, depth_step, chan_of):
    depth, chans = lax.axis_size("space"), lax.axis_size("chan")
    route = []
    for s in range(depth):
        for c in range(chans):
            to = chan_of(c)
            if 0 <= s + depth_step < depth and 0 <= to < chans:
                route.append((s * chans + c, (s + depth_step) * chans + to))
    return lax.ppermute(block, BOTH, route)


def gathered(own, first, last, meanwhile=None):
    across = [moved(part, 0, lambda c: c ^ 2) for part in own]
    up = moved(last, 1, lambda c: c)
    down = moved(first, -1, lambda c: c)
    core = [moved(part, 0, lambda c: c ^ 1) for part in own]
    rim = jnp.concatenate([up, down], 0)
    across_rim = moved(rim, 0, lambda c: c ^ 2)
    across, held, meanwhile = lax.optimization_barrier((across, rim, meanwhile))
    core_rim = moved(held, 0, lambda c: c ^ 1)
    pair = [moved(piece, 0, lambda c: c ^ 1) for piece in (*across, across_rim)]
    blocks = [*own, rim, *core, core_rim, *across, across_rim, *pair]
    return blocks if meanwhile is None else (blocks, meanwhile)


def summed(parts):
    terms = lax.all_to_all(parts, "space", 0, 0)
    own = jnp.sum(terms.astype(F32), 0)
    shape = own.shape
    row = lax.broadcasted_iota(jnp.int32, shape, 0)
    shared = (row >= 32) & (lane_of(shape) >= 128) | (lax.axis_index("space") == 27)
    both = own
    for step in (1, 2):
        sent = lax.optimization_barrier(both.astype(BF))
        both = sent.astype(F32) + moved(sent, 0, lambda c, step=step: c ^ step).astype(F32)
    total = jnp.where(shared, both, own).astype(BF)
    return lax.all_to_all(jnp.broadcast_to(total[None], parts.shape), "space", 0, 0)


def per_device(volume, kernel_one, kernel_two, kernel_three, kernel_four, cotangent):
    me = lax.axis_index("chan").astype(jnp.int32)[None]
    below = moved(volume[:, :3], -1, lambda c: c)
    beside = moved(volume[:, :, :3], 0, lambda c: c - 1)
    corner = moved(volume[:, :3, :3], -1, lambda c: c - 1)

    three = jnp.pad(kernel_three.reshape(27, 16, 128), ((0, 0), (0, 0), (0, 128)))
    four = kernel_four.reshape(27, 32, 256)
    filters = lax.all_gather(jnp.concatenate([four, three], 1), "chan")
    cotangent = jnp.transpose(cotangent.reshape(64, 4, 1024), (1, 0, 2))
    corner, cotangent = lax.optimization_barrier((corner, cotangent))

    even = jnp.pad(kernel_one, ((0, 0), (0, 0), (0, 5), (0, 0), (0, 0)))
    odd = jnp.pad(kernel_one, ((0, 0), (0, 0), (2, 3), (0, 0), (0, 0)))
    w_one = jnp.stack([even, odd]).reshape(2, 288, 32).transpose(0, 2, 1).reshape(64, 288)
    w_two = kernel_two.reshape(864, 64).T
    top = jnp.concatenate([kernel_two[:, :, 0], kernel_two[:, :, 2]], 3)
    bottom = jnp.pad(kernel_two[:, :, 1], ((0, 0), (0, 0), (0, 0), (0, 64)))
    w_back = jnp.concatenate([top, bottom], 2).reshape(9, 64, 128)

    tall = jnp.concatenate([volume, below], 1)
    side = jnp.pad(jnp.concatenate([beside, corner], 1), ((0, 0), (0, 0), (0, 5), (0, 0)))
    tall = jnp.concatenate([tall, side], 2)

    field, act_one, slope_one, body, first, last, slope_two = call(
        first_layers_kernel,
        [
            ((19, 352, 128), BF),
            ((9, 480, 128), BF),
            ((8, 64, 512), F32),
            ((4, 64, 384), BF),
            ((1, 64, 512), BF),
            ((1, 64, 512), BF),
            ((4, 64, 256), F32),
        ],
        [tall, w_one, w_two],
        [((19, 352, 128), BF), ((9, 480, 128), BF), ((8, 64, 512), F32)],
        away=(0, 1, 2),
    )
    pieces = range(1, 9)
    (w_three,) = call(
        turn_kernel, [((96, 576), BF)], [me, filters], [((4, 27, 16, 128), BF)], anywhere=(1,), far=(1,)
    )
    blocks, w_three = gathered([body], first, last, w_three)
    act_three, first, last, slope_three, own_two, front, row = call(
        third_kernel,
        [((4, 32, 1024), BF), ((1, 32, 1024), BF), ((1, 32, 1024), BF), ((4, 32, 1024), F32), ((6, 16, 1280), BF), ((64, 384), BF), ((4, 64, 128), BF)],
        [me, *blocks, w_three],
        [((6, 64, 1280), BF), ((4, 32, 1024), F32), ((64, 384), BF), ((4, 64, 128), BF)],
        anywhere=pieces,
        away=(3, 4, 5, 6),
    )
    blocks = gathered([act_three], first, last)
    features, back_four, first, last = call(
        fourth_kernel,
        [((4, 64, 1024), BF), ((4, 64, 1024), BF), ((1, 64, 1024), BF), ((1, 64, 1024), BF)],
        [me, *blocks, filters, cotangent],
        [((6, 128, 1280), BF)],
        anywhere=pieces,
    )
    features = jnp.transpose(features, (1, 0, 2)).reshape(64, 4, 8, 128)
    all_four = gathered([back_four], first, last)
    back_three, first, last = call(
        into_three_kernel,
        [((4, 32, 1024), BF), ((1, 32, 1024), BF), ((2, 32, 1024), BF)],
        [me, *all_four, four, slope_three],
        [((6, 256, 1280), BF)],
        anywhere=pieces,
    )
    (grad_four,) = call(
        grad_four_kernel,
        [((864, 256), BF)],
        [me, *blocks[:2], *all_four[::2]],
        [((6, 96, 1280), BF), ((4, 256, 1024), BF)],
        flops=2 * 864 * 256 * 4096,
        anywhere=range(3, 7),
    )
    blocks, grad_four = gathered([back_three], first, last, grad_four)
    (grads,) = call(
        last_kernel,
        [((32, 48, 256), BF)],
        [
            me,
            *blocks,
            filters,
            w_back,
            own_two,
            grad_four.reshape(27, 32, 256),
            slope_two,
            front,
            row,
            act_one,
            slope_one,
            field,
        ],
        [
            ((7, 128, 1408), BF),
            ((6, 48, 1280), BF),
            ((5, 3, 128, 128), BF),
            ((8, 64, 512), BF),
        ],
        anywhere=pieces,
    )
    grad_one, grad_two, grad_three, grad_four = call(
        unpack_kernel,
        [((3, 3, 3, 4, 32), F32), ((864, 64), F32), ((27, 16, 128), F32), ((27, 32, 256), F32)],
        [summed(grads)],
        [((1152, 64), F32)],
    )
    grad_two = grad_two.reshape(3, 3, 3, 32, 64)
    grad_three = grad_three.reshape(3, 3, 3, 16, 128)
    grad_four = grad_four.reshape(3, 3, 3, 32, 256)
    return (features, grad_one, grad_two, grad_three, grad_four)


def solution(mesh):
    in_specs = (
        P(None, "space", "chan", None),
        P(),
        P(),
        P(None, None, None, "chan", None),
        P(None, None, None, "chan", None),
        P("chan", "space", None, None),
    )
    out_specs = (
        P("chan", "space", None, None),
        P(),
        P(),
        P(None, None, None, "chan", None),
        P(None, None, None, "chan", None),
    )
    return jax.shard_map(
        per_device, mesh=mesh, in_specs=in_specs, out_specs=out_specs, check_vma=False
    )
```

```python
import jax
import jax.numpy as jnp
import numpy as np
from jax import lax
from jax.experimental import pallas as pl
from jax.experimental.pallas import tpu as pltpu
from jax.sharding import PartitionSpec as P

BF = jnp.bfloat16
F32 = jnp.float32
BOTH = ("space", "chan")
LANES = 128
VMEM_LIMIT = 20 * 1024 * 1024


def mm(left, right):
    return lax.dot_general(left, right, (((1,), (0,)), ((), ())), preferred_element_type=F32)


def mm_nt(left, right):
    return lax.dot_general(left, right, (((1,), (1,)), ((), ())), preferred_element_type=F32)


def lane_of(shape):
    return lax.broadcasted_iota(jnp.int32, shape, len(shape) - 1)


def shifted(value, step):
    width = value.shape[1]
    turned = pltpu.roll(value, step % width, 1)
    edge = 0 if step == 1 else LANES - 1
    return jnp.where(lane_of(value.shape) % LANES == edge, 0.0, turned)


def activate(pre):
    sigma = jax.nn.sigmoid(pre)
    return pre * sigma, sigma * (1.0 + pre * (1.0 - sigma))


def call(kernel, outs, args, scratch=(), flops=0, anywhere=(), away=(), far=()):
    specs = []
    for place, a in enumerate(args):
        space = pltpu.SMEM if a.dtype == jnp.int32 else pltpu.VMEM
        specs.append(pl.BlockSpec(memory_space=pl.ANY if place in anywhere else space))
    size = sum(a.size * a.dtype.itemsize for a in args)
    args = [pltpu.with_memory_space_constraint(a, pltpu.HBM) if place in far else a for place, a in enumerate(args)]
    size += sum(int(np.prod(s)) * jnp.dtype(t).itemsize for s, t in outs)
    buffers = [pltpu.VMEM(s, t) for s, t in scratch]
    buffers.append(pltpu.SemaphoreType.DMA((28,)))
    places = [pltpu.HBM if place in away else pltpu.VMEM for place in range(len(outs))]
    return pl.pallas_call(
        kernel,
        out_shape=[
            pltpu.HBM(s, t) if place in away else jax.ShapeDtypeStruct(s, t)
            for place, (s, t) in enumerate(outs)
        ],
        in_specs=specs,
        out_specs=[pl.BlockSpec(memory_space=place) for place in places],
        scratch_shapes=buffers,
        compiler_params=pltpu.CompilerParams(vmem_limit_bytes=VMEM_LIMIT),
        cost_estimate=pl.CostEstimate(flops=flops, bytes_accessed=size, transcendentals=0),
    )(*args)


def begin(source, target, sem):
    copy = pltpu.make_async_copy(source, target, sem)
    copy.start()
    return copy


def picks(shape, column_of):
    row = lax.broadcasted_iota(jnp.int32, shape, 0)
    return jnp.where(column_of(row, lane_of(shape)), 1.0, 0.0).astype(BF)


def phase_matrix():
    return picks((512, 640), lambda row, lane: row == 4 * (lane % 128) + lane // 128)


def row_matrix():
    def at(row, lane):
        return lane == row // 4 % 8 * 64 + row % 4 * 16 + row // 32

    return picks((352, 320), at)


def first_layers_kernel(vol, w_one, w_two, *refs):
    field_out, act_one_out, slope_one_out, body, first, last, slope_two = refs[:7]
    field, act_one, slope_one, sems = refs[7:]
    phases = phase_matrix()
    rows = row_matrix()
    for start in range(0, 19, 4):
        planes = range(start, min(start + 4, 19))
        block = jnp.concatenate([jnp.reshape(vol[:, d], (64, 512)) for d in planes], 0)
        split = mm(block, phases).astype(BF)
        columns = []
        for n in range(len(planes)):
            parts = [split[n * 64 : n * 64 + 64, p * 128 : p * 128 + 128] for p in range(5)]
            columns.append(jnp.concatenate(parts, 0))
        placed = mm(rows, jnp.concatenate(columns, 1)).astype(BF)
        for n, d in enumerate(planes):
            field[d] = placed[:, n * 128 : n * 128 + 128]
    leaving = [begin(field, field_out, sems.at[0])]
    for d in range(9):
        columns = []
        for h in range(5):
            parts = [field[2 * d + a, h * 64 : h * 64 + 96] for a in range(3)]
            columns.append(jnp.concatenate(parts, 0))
        pre = mm(w_one[...], jnp.concatenate(columns, 1))
        act, slope = activate(pre)
        if d < 8:
            slope_one[d] = slope[:, :512]
        beside = shifted(act[:32], -1)
        for h in range(5):
            lanes = slice(h * 128, h * 128 + 128)
            act_one[d, h * 96 : h * 96 + 64] = act[:, lanes].astype(BF)
            act_one[d, h * 96 + 64 : h * 96 + 96] = beside[:, lanes].astype(BF)
    leaving.append(begin(slope_one, slope_one_out, sems.at[1]))
    leaving.append(begin(act_one, act_one_out, sems.at[2]))
    for d in range(4):
        columns = []
        for h in range(2):
            parts = [act_one[2 * d + a, h * 192 : h * 192 + 288] for a in range(3)]
            columns.append(jnp.concatenate(parts, 0))
        pre = mm(w_two[...], jnp.concatenate(columns, 1))
        act, slope = activate(pre)
        slope_two[d] = slope
        steep = slope.astype(BF)
        body[d, :, :256] = act.astype(BF)
        body[d, :, 256:] = steep[:, 128:]
        if d == 0:
            first[0] = act.astype(BF)
        if d == 3:
            last[0] = act.astype(BF)
            last[1] = steep
    for copy in leaving:
        copy.wait()


def turned(me, blocks, count):
    wide = 4 * count
    row = lax.broadcasted_iota(jnp.int32, (count, wide), 0)
    pick = jnp.where(lane_of((count, wide)) == row + me * count, 1.0, 0.0).astype(BF)
    parts = []
    for c in range(3):
        rows = [blocks[j, ab * 3 + c] for ab in range(9) for j in range(4)]
        parts.append(mm_nt(pick, jnp.concatenate(rows, 0)).astype(BF))
    return jnp.concatenate(parts, 0)


def taps_of(field, d, start, width):
    parts = []
    for a in range(3):
        for b in range(3):
            parts.append(field[d + a, :, pl.ds(start + b * LANES, width)])
    return jnp.concatenate(parts, 0)


def shift_sum(product, channels):
    low = product[:channels]
    mid = product[channels : 2 * channels]
    high = product[2 * channels :]
    return shifted(low, 1) + mid + shifted(high, -1)


def clear_rims(field):
    depth, channels, lanes = field.shape
    rim = jnp.zeros((depth, channels, LANES), BF)
    field[:, :, :LANES] = rim
    field[:, :, lanes - LANES :] = rim


def arrive(refs, sems, target, up=1, width=1024):
    parts = len(refs) // 4 - 1
    copies = []
    for k in range(4):
        *bodies, rim = refs[k * (parts + 1) : (k + 1) * (parts + 1)]
        lanes = pl.ds(0, width)
        planes = 4 // parts
        pieces = [(body.at[:, :, lanes], up + n * planes, planes) for n, body in enumerate(bodies)]
        pieces.append((rim.at[pl.ds(0, up), :, lanes], 0, up))
        pieces.append((rim.at[pl.ds(rim.shape[0] - 1, 1), :, lanes], up + 4, 1))
        for n, (source, first, count) in enumerate(pieces):
            copies.append(pltpu.make_async_copy(source, target(k, first, count), sems.at[4 * k + n]))
    for copy in copies:
        copy.start()
    return copies


def assemble(field, me, refs, sems, channels, up=1, rim=1):
    def target(k, first, count):
        at = pl.multiple_of((me ^ k) * channels, channels)
        return field.at[pl.ds(first, count), pl.ds(at, channels), pl.ds(rim * LANES, 8 * LANES)]

    return arrive(refs, sems, target, up)


def turn_kernel(me_ref, filters, weights, kernel, sems):
    arrived = begin(filters.at[:, :, pl.ds(32, 16), pl.ds(0, LANES)], kernel, sems.at[0])
    arrived.wait()
    weights[...] = turned(me_ref[0], kernel, 32)


def third_kernel(me_ref, *refs):
    blocks, weights = refs[:8], refs[8]
    act, first, last, slope_out, own_out, front_out, row_out = refs[9:16]
    field, slope, front, row, sems = refs[16:]
    me = me_ref[0]

    def target(k, first, count):
        at = pl.multiple_of(LANES + (me ^ k) * (2 * LANES), LANES)
        return field.at[pl.ds(first, count), :, pl.ds(at, 2 * LANES)]

    copies = arrive(blocks, sems, target, 1, 2 * LANES)
    plane = begin(blocks[1].at[1], front.at[:, pl.ds(LANES, 256)], sems.at[21])

    @pl.when(me == 0)
    def _():
        front[:, :LANES] = jnp.zeros((64, LANES), BF)
        row[...] = jnp.zeros((4, 64, LANES), BF)

    for k in (1, 3):

        @pl.when((me > 0) & (me ^ k == me - 1))
        def _(k=k):
            begin(blocks[2 * k + 1].at[1, :, pl.ds(LANES, LANES)], front.at[:, pl.ds(0, LANES)], sems.at[22])
            begin(blocks[2 * k].at[:, :, pl.ds(256, LANES)], row, sems.at[23])

    clear_rims(field)
    plane.wait()

    @pl.when(me > 0)
    def _():
        corner = blocks[1].at[1, :, pl.ds(LANES, LANES)]
        pltpu.make_async_copy(corner, front.at[:, pl.ds(0, LANES)], sems.at[22]).wait()
        pltpu.make_async_copy(blocks[0].at[:, :, pl.ds(256, LANES)], row, sems.at[23]).wait()

    leaving = [begin(front, front_out, sems.at[24]), begin(row, row_out, sems.at[25])]
    for copy in copies:
        copy.wait()
    own = field.at[:, pl.ds(pl.multiple_of(me * 16, 16), 16), :]
    leaving.append(begin(own, own_out, sems.at[26]))
    for d in range(4):
        product = mm(weights[...], taps_of(field, d, 0, 1024))
        value, steep = activate(shift_sum(product, 32))
        act[d] = value.astype(BF)
        slope[d] = steep
    first[0] = act[0]
    last[0] = act[3]
    leaving.append(begin(slope, slope_out, sems.at[27]))
    for copy in leaving:
        copy.wait()


def fourth_kernel(me_ref, *refs):
    blocks, filters, cotangent = refs[:8], refs[8], refs[9]
    features, back, first, last, field, sems = refs[10:]
    me = me_ref[0]
    copies = assemble(field, me, blocks, sems, 32)
    clear_rims(field)
    weights = turned(me, filters.at[:, :, :32], 64)
    for copy in copies:
        copy.wait()
    for d in range(4):
        product = mm(weights, taps_of(field, d, 0, 1024))
        value, steep = activate(shift_sum(product, 64))
        features[d] = value.astype(BF)
        back[d] = (cotangent[d].astype(F32) * steep).astype(BF)
    first[0] = back[0]
    last[0] = back[3]


def flipped_weights(kernel):
    columns = []
    for a in range(3):
        for b in range(3):
            taps = [((2 - a) * 3 + 2 - b) * 3 + 2 - c for c in range(3)]
            columns.append(jnp.concatenate([kernel[t] for t in taps], 0))
    return jnp.concatenate(columns, 1)


def into_three_kernel(me_ref, *refs):
    blocks, kernel, slope = refs[:8], refs[8], refs[9]
    back, first, last, field, sems = refs[10:]
    copies = assemble(field, me_ref[0], blocks, sems, 64)
    clear_rims(field)
    weights = flipped_weights(kernel)
    for copy in copies:
        copy.wait()
    for d in range(4):
        product = mm(weights, taps_of(field, d, 0, 1024))
        back[d] = (shift_sum(product, 32) * slope[d]).astype(BF)
    first[0] = back[0]
    last[...] = back[2:]


def three_shifts(value):
    wide = value.astype(F32)
    return jnp.concatenate([shifted(wide, 1).astype(BF), value, shifted(wide, -1).astype(BF)], 0)


def filter_grad(wide, gradients):
    total = None
    for d in range(4):
        term = mm_nt(taps_of(wide, d, 0, 1024), gradients(d))
        total = term if total is None else total + term
    return total


def grad_four_kernel(me_ref, own, rim, *refs):
    blocks, grad, wide, gradient, sems = refs[:4], *refs[4:]
    copies = []
    for k in range(4):
        at = pl.multiple_of((me_ref[0] ^ k) * 64, 64)
        copies.append(begin(blocks[k], gradient.at[:, pl.ds(at, 64), :], sems.at[k]))
    clear_rims(wide)
    inside = slice(LANES, 9 * LANES)
    wide[0, :, inside] = three_shifts(rim[0])
    for d in range(4):
        wide[d + 1, :, inside] = three_shifts(own[d])
    wide[5, :, inside] = three_shifts(rim[1])
    for copy in copies:
        copy.wait()
    grad[...] = filter_grad(wide, lambda d: gradient[d]).astype(BF)


def last_kernel(me_ref, *refs):
    blocks = refs[:8]
    filters, w_back, act_two, grad_four = refs[8:12]
    slope, front, row, act_one, slope_one, volume = refs[12:18]
    out, field, shifts, wide, back_one, sems = refs[18:]
    me = me_ref[0]
    copies = assemble(field, me, blocks, sems, 32, up=2, rim=2)
    field[:, :, : 2 * LANES] = jnp.zeros((7, 128, 2 * LANES), BF)
    field[:, :, 10 * LANES :] = jnp.zeros((7, 128, LANES), BF)
    clear_rims(shifts)
    inside = slice(LANES, 9 * LANES)
    for d in range(6):
        shifts[d, :, inside] = three_shifts(act_two[d, :, inside])
    for t in range(27):
        out[t, :32] = grad_four[t]
    for t in range(27, 32):
        out[t] = jnp.zeros((48, 256), BF)
    taps = [jnp.concatenate([filters[j, t, 32:, :LANES] for j in range(4)], 0) for t in range(27)]
    weights = flipped_weights(taps)
    for copy in copies:
        copy.wait()

    start = pl.multiple_of(me * (2 * LANES), LANES)
    for d in range(5):
        steep = front[...].astype(F32)
        if d > 0:
            steep = jnp.concatenate([row[d - 1].astype(F32), slope[d - 1]], 1)
        product = mm(weights, taps_of(field, d, start, 3 * LANES))
        value = shift_sum(product, 64) * steep
        value = value.astype(BF)
        beside = shifted(value.astype(F32), 1).astype(BF)
        for h in range(3):
            wide[d, h, :64] = value[:, h * 128 : h * 128 + 128]
            wide[d, h, 64:] = beside[:, h * 128 : h * 128 + 128]
    for d_odd in range(2):
        for h_odd in range(2):
            taps = [(a, b) for a in ((1,) if d_odd else (0, 2)) for b in ((1,) if h_odd else (0, 2))]
            mixed = jnp.concatenate([w_back[a * 3 + b] for a, b in taps], 1)
            columns = []
            for d in range(4):
                for h in range(2):
                    parts = [wide[d + 1 - a // 2, h + 1 - b // 2] for a, b in taps]
                    columns.append(jnp.concatenate(parts, 0))
            into = mm(mixed, jnp.concatenate(columns, 1))
            for d in range(4):
                for h in range(2):
                    at = (d * 2 + h) * 128
                    lanes = slice((2 * h + h_odd) * 128, (2 * h + h_odd) * 128 + 128)
                    d_one = 2 * d + d_odd
                    value = into[:, at : at + 128] * slope_one[d_one, :, lanes]
                    back_one[d_one, :, lanes] = value.astype(BF)
    three = filter_grad(shifts, lambda d: field[d + 2, :, 2 * LANES : 10 * LANES]).astype(BF)
    for t in range(27):
        out[t, 32:, :128] = three[t * 16 : t * 16 + 16]
    two = None
    for d in range(4):
        columns = []
        for h in range(2):
            parts = [act_one[2 * d + a, h * 192 : h * 192 + 288] for a in range(3)]
            columns.append(jnp.concatenate(parts, 0))
        own = jnp.concatenate([wide[d + 1, 1, :64], wide[d + 1, 2, :64]], 1)
        term = mm_nt(jnp.concatenate(columns, 1), own)
        two = term if two is None else two + term
    one = None
    for d in range(8):
        columns = []
        for h in range(4):
            parts = [volume[2 * d + a, h * 64 : h * 64 + 96] for a in range(3)]
            columns.append(jnp.concatenate(parts, 0))
        term = mm_nt(jnp.concatenate(columns, 1), back_one[d])
        one = term if one is None else one + term
    both = jnp.concatenate([two, one], 0)
    for t in range(32):
        pair = [both[32 * t + 16 * q : 32 * t + 16 * q + 16] for q in range(2)]
        out[t, 32:, 128:] = jnp.concatenate(pair, 1).astype(BF)
    rest = [both[1024 + 32 * q : 1056 + 32 * q] for q in range(4)]
    out[27, :32] = jnp.concatenate(rest, 1).astype(BF)


def unpack_kernel(packed, grad_one, grad_two, grad_three, grad_four, both, sems):
    for t in range(27):
        grad_four[t] = packed[t, :32].astype(F32)
        grad_three[t] = packed[t, 32:, :128].astype(F32)
    for t in range(32):
        pair = packed[t, 32:, 128:].astype(F32)
        both[32 * t : 32 * t + 16] = pair[:, :64]
        both[32 * t + 16 : 32 * t + 32] = pair[:, 64:]
    rest = packed[27, :32].astype(F32)
    for q in range(4):
        both[1024 + 32 * q : 1056 + 32 * q] = rest[:, 64 * q : 64 * q + 64]
    grad_two[...] = both[:864]
    for t in range(9):
        at = 864 + 32 * t
        value = both[at : at + 12, :32] + both[at + 8 : at + 20, 32:]
        for c in range(3):
            grad_one[t // 3, t % 3, c] = value[4 * c : 4 * c + 4]


def moved(block, depth_step, chan_of):
    depth, chans = lax.axis_size("space"), lax.axis_size("chan")
    route = []
    for s in range(depth):
        for c in range(chans):
            to = chan_of(c)
            if 0 <= s + depth_step < depth and 0 <= to < chans:
                route.append((s * chans + c, (s + depth_step) * chans + to))
    return lax.ppermute(block, BOTH, route)


def gathered(own, first, last, meanwhile=None):
    across = [moved(part, 0, lambda c: c ^ 2) for part in own]
    up = moved(last, 1, lambda c: c)
    down = moved(first, -1, lambda c: c)
    core = [moved(part, 0, lambda c: c ^ 1) for part in own]
    rim = jnp.concatenate([up, down], 0)
    across_rim = moved(rim, 0, lambda c: c ^ 2)
    across, held, meanwhile = lax.optimization_barrier((across, rim, meanwhile))
    core_rim = moved(held, 0, lambda c: c ^ 1)
    pair = [moved(piece, 0, lambda c: c ^ 1) for piece in (*across, across_rim)]
    blocks = [*own, rim, *core, core_rim, *across, across_rim, *pair]
    return blocks if meanwhile is None else (blocks, meanwhile)


def summed(parts):
    terms = lax.all_to_all(parts, "space", 0, 0)
    own = jnp.sum(terms.astype(F32), 0)
    shape = own.shape
    row = lax.broadcasted_iota(jnp.int32, shape, 0)
    shared = (row >= 32) & (lane_of(shape) >= 128) | (lax.axis_index("space") == 27)
    both = own
    for step in (1, 2):
        sent = lax.optimization_barrier(both.astype(BF))
        both = sent.astype(F32) + moved(sent, 0, lambda c, step=step: c ^ step).astype(F32)
    total = jnp.where(shared, both, own).astype(BF)
    return lax.all_to_all(jnp.broadcast_to(total[None], parts.shape), "space", 0, 0)


def per_device(volume, kernel_one, kernel_two, kernel_three, kernel_four, cotangent):
    me = lax.axis_index("chan").astype(jnp.int32)[None]
    below = moved(volume[:, :3], -1, lambda c: c)
    beside = moved(volume[:, :, :3], 0, lambda c: c - 1)
    corner = moved(volume[:, :3, :3], -1, lambda c: c - 1)

    three = jnp.pad(kernel_three.reshape(27, 16, 128), ((0, 0), (0, 0), (0, 128)))
    four = kernel_four.reshape(27, 32, 256)
    filters = lax.all_gather(jnp.concatenate([four, three], 1), "chan")
    cotangent = jnp.transpose(cotangent.reshape(64, 4, 1024), (1, 0, 2))
    corner, cotangent = lax.optimization_barrier((corner, cotangent))

    even = jnp.pad(kernel_one, ((0, 0), (0, 0), (0, 5), (0, 0), (0, 0)))
    odd = jnp.pad(kernel_one, ((0, 0), (0, 0), (2, 3), (0, 0), (0, 0)))
    w_one = jnp.stack([even, odd]).reshape(2, 288, 32).transpose(0, 2, 1).reshape(64, 288)
    w_two = kernel_two.reshape(864, 64).T
    top = jnp.concatenate([kernel_two[:, :, 0], kernel_two[:, :, 2]], 3)
    bottom = jnp.pad(kernel_two[:, :, 1], ((0, 0), (0, 0), (0, 0), (0, 64)))
    w_back = jnp.concatenate([top, bottom], 2).reshape(9, 64, 128)

    tall = jnp.concatenate([volume, below], 1)
    side = jnp.pad(jnp.concatenate([beside, corner], 1), ((0, 0), (0, 0), (0, 5), (0, 0)))
    tall = jnp.concatenate([tall, side], 2)

    field, act_one, slope_one, body, first, last, slope_two = call(
        first_layers_kernel,
        [
            ((19, 352, 128), BF),
            ((9, 480, 128), BF),
            ((8, 64, 512), F32),
            ((4, 64, 384), BF),
            ((1, 64, 256), BF),
            ((2, 64, 256), BF),
            ((4, 64, 256), F32),
        ],
        [tall, w_one, w_two],
        [((19, 352, 128), BF), ((9, 480, 128), BF), ((8, 64, 512), F32)],
        away=(0, 1, 2),
    )
    pieces = range(1, 9)
    (w_three,) = call(
        turn_kernel, [((96, 576), BF)], [me, filters], [((4, 27, 16, 128), BF)], anywhere=(1,), far=(1,)
    )
    blocks, w_three = gathered([body], first, last, w_three)
    act_three, first, last, slope_three, own_two, front, row = call(
        third_kernel,
        [((4, 32, 1024), BF), ((1, 32, 1024), BF), ((1, 32, 1024), BF), ((4, 32, 1024), F32), ((6, 16, 1280), BF), ((64, 384), BF), ((4, 64, 128), BF)],
        [me, *blocks, w_three],
        [((6, 64, 1280), BF), ((4, 32, 1024), F32), ((64, 384), BF), ((4, 64, 128), BF)],
        anywhere=pieces,
        away=(3, 4, 5, 6),
    )
    blocks = gathered([act_three], first, last)
    features, back_four, first, last = call(
        fourth_kernel,
        [((4, 64, 1024), BF), ((4, 64, 1024), BF), ((1, 64, 1024), BF), ((1, 64, 1024), BF)],
        [me, *blocks, filters, cotangent],
        [((6, 128, 1280), BF)],
        anywhere=pieces,
    )
    features = jnp.transpose(features, (1, 0, 2)).reshape(64, 4, 8, 128)
    all_four = gathered([back_four], first, last)
    back_three, first, last = call(
        into_three_kernel,
        [((4, 32, 1024), BF), ((1, 32, 1024), BF), ((2, 32, 1024), BF)],
        [me, *all_four, four, slope_three],
        [((6, 256, 1280), BF)],
        anywhere=pieces,
    )
    (grad_four,) = call(
        grad_four_kernel,
        [((864, 256), BF)],
        [me, *blocks[:2], *all_four[::2]],
        [((6, 96, 1280), BF), ((4, 256, 1024), BF)],
        flops=2 * 864 * 256 * 4096,
        anywhere=range(3, 7),
    )
    blocks, grad_four = gathered([back_three], first, last, grad_four)
    (grads,) = call(
        last_kernel,
        [((32, 48, 256), BF)],
        [
            me,
            *blocks,
            filters,
            w_back,
            own_two,
            grad_four.reshape(27, 32, 256),
            slope_two,
            front,
            row,
            act_one,
            slope_one,
            field,
        ],
        [
            ((7, 128, 1408), BF),
            ((6, 48, 1280), BF),
            ((5, 3, 128, 128), BF),
            ((8, 64, 512), BF),
        ],
        anywhere=pieces,
    )
    grad_one, grad_two, grad_three, grad_four = call(
        unpack_kernel,
        [((3, 3, 3, 4, 32), F32), ((864, 64), F32), ((27, 16, 128), F32), ((27, 32, 256), F32)],
        [summed(grads)],
        [((1152, 64), F32)],
    )
    grad_two = grad_two.reshape(3, 3, 3, 32, 64)
    grad_three = grad_three.reshape(3, 3, 3, 16, 128)
    grad_four = grad_four.reshape(3, 3, 3, 32, 256)
    return (features, grad_one, grad_two, grad_three, grad_four)


def solution(mesh):
    in_specs = (
        P(None, "space", "chan", None),
        P(),
        P(),
        P(None, None, None, "chan", None),
        P(None, None, None, "chan", None),
        P("chan", "space", None, None),
    )
    out_specs = (
        P("chan", "space", None, None),
        P(),
        P(),
        P(None, None, None, "chan", None),
        P(None, None, None, "chan", None),
    )
    return jax.shard_map(
        per_device, mesh=mesh, in_specs=in_specs, out_specs=out_specs, check_vma=False
    )
```

```python
import jax
import jax.numpy as jnp
import numpy as np
from jax import lax
from jax.experimental import pallas as pl
from jax.experimental.pallas import tpu as pltpu
from jax.sharding import PartitionSpec as P

BF = jnp.bfloat16
F32 = jnp.float32
BOTH = ("space", "chan")
LANES = 128
VMEM_LIMIT = 14 * 1024 * 1024


def mm(left, right):
    return lax.dot_general(left, right, (((1,), (0,)), ((), ())), preferred_element_type=F32)


def mm_nt(left, right):
    return lax.dot_general(left, right, (((1,), (1,)), ((), ())), preferred_element_type=F32)


def lane_of(shape):
    return lax.broadcasted_iota(jnp.int32, shape, len(shape) - 1)


def shifted(value, step):
    width = value.shape[1]
    turned = pltpu.roll(value, step % width, 1)
    edge = 0 if step == 1 else LANES - 1
    return jnp.where(lane_of(value.shape) % LANES == edge, 0.0, turned)


def activate(pre):
    sigma = jax.nn.sigmoid(pre)
    return pre * sigma, sigma * (1.0 + pre * (1.0 - sigma))


def call(kernel, outs, args, scratch=(), flops=0, anywhere=(), away=(), far=()):
    specs = []
    for place, a in enumerate(args):
        space = pltpu.SMEM if a.dtype == jnp.int32 else pltpu.VMEM
        specs.append(pl.BlockSpec(memory_space=pl.ANY if place in anywhere else space))
    size = sum(a.size * a.dtype.itemsize for a in args)
    args = [pltpu.with_memory_space_constraint(a, pltpu.HBM) if place in far else a for place, a in enumerate(args)]
    size += sum(int(np.prod(s)) * jnp.dtype(t).itemsize for s, t in outs)
    buffers = [pltpu.VMEM(s, t) for s, t in scratch]
    buffers.append(pltpu.SemaphoreType.DMA((28,)))
    places = [pltpu.HBM if place in away else pltpu.VMEM for place in range(len(outs))]
    return pl.pallas_call(
        kernel,
        out_shape=[
            pltpu.HBM(s, t) if place in away else jax.ShapeDtypeStruct(s, t)
            for place, (s, t) in enumerate(outs)
        ],
        in_specs=specs,
        out_specs=[pl.BlockSpec(memory_space=place) for place in places],
        scratch_shapes=buffers,
        compiler_params=pltpu.CompilerParams(vmem_limit_bytes=VMEM_LIMIT),
        cost_estimate=pl.CostEstimate(flops=flops, bytes_accessed=size, transcendentals=0),
    )(*args)


def begin(source, target, sem):
    copy = pltpu.make_async_copy(source, target, sem)
    copy.start()
    return copy


def picks(shape, column_of):
    row = lax.broadcasted_iota(jnp.int32, shape, 0)
    return jnp.where(column_of(row, lane_of(shape)), 1.0, 0.0).astype(BF)


def phase_matrix():
    return picks((512, 640), lambda row, lane: row == 4 * (lane % 128) + lane // 128)


def row_matrix():
    def at(row, lane):
        return lane == row // 4 % 8 * 64 + row % 4 * 16 + row // 32

    return picks((352, 320), at)


def first_layers_kernel(vol, w_one, w_two, *refs):
    field_out, act_one_out, slope_one_out, body, first, last, slope_two = refs[:7]
    field, act_one, slope_one, sems = refs[7:]
    phases = phase_matrix()
    rows = row_matrix()
    for start in range(0, 19, 4):
        planes = range(start, min(start + 4, 19))
        block = jnp.concatenate([jnp.reshape(vol[:, d], (64, 512)) for d in planes], 0)
        split = mm(block, phases).astype(BF)
        columns = []
        for n in range(len(planes)):
            parts = [split[n * 64 : n * 64 + 64, p * 128 : p * 128 + 128] for p in range(5)]
            columns.append(jnp.concatenate(parts, 0))
        placed = mm(rows, jnp.concatenate(columns, 1)).astype(BF)
        for n, d in enumerate(planes):
            field[d] = placed[:, n * 128 : n * 128 + 128]
    leaving = [begin(field, field_out, sems.at[0])]
    for d in range(9):
        columns = []
        for h in range(5):
            parts = [field[2 * d + a, h * 64 : h * 64 + 96] for a in range(3)]
            columns.append(jnp.concatenate(parts, 0))
        pre = mm(w_one[...], jnp.concatenate(columns, 1))
        act, slope = activate(pre)
        if d < 8:
            slope_one[d] = slope[:, :512]
        beside = shifted(act[:32], -1)
        for h in range(5):
            lanes = slice(h * 128, h * 128 + 128)
            act_one[d, h * 96 : h * 96 + 64] = act[:, lanes].astype(BF)
            act_one[d, h * 96 + 64 : h * 96 + 96] = beside[:, lanes].astype(BF)
    leaving.append(begin(slope_one, slope_one_out, sems.at[1]))
    leaving.append(begin(act_one, act_one_out, sems.at[2]))
    for d in range(4):
        columns = []
        for h in range(2):
            parts = [act_one[2 * d + a, h * 192 : h * 192 + 288] for a in range(3)]
            columns.append(jnp.concatenate(parts, 0))
        pre = mm(w_two[...], jnp.concatenate(columns, 1))
        act, slope = activate(pre)
        slope_two[d] = slope
        steep = slope.astype(BF)
        body[d, :, :256] = act.astype(BF)
        body[d, :, 256:] = steep[:, 128:]
        if d == 0:
            first[0] = act.astype(BF)
        if d == 3:
            last[0] = act.astype(BF)
            last[1] = steep
    for copy in leaving:
        copy.wait()


def turned(me, blocks, count):
    wide = 4 * count
    row = lax.broadcasted_iota(jnp.int32, (count, wide), 0)
    pick = jnp.where(lane_of((count, wide)) == row + me * count, 1.0, 0.0).astype(BF)
    parts = []
    for c in range(3):
        rows = [blocks[j, ab * 3 + c] for ab in range(9) for j in range(4)]
        parts.append(mm_nt(pick, jnp.concatenate(rows, 0)).astype(BF))
    return jnp.concatenate(parts, 0)


def taps_of(field, d, start, width):
    parts = []
    for a in range(3):
        for b in range(3):
            parts.append(field[d + a, :, pl.ds(start + b * LANES, width)])
    return jnp.concatenate(parts, 0)


def shift_sum(product, channels):
    low = product[:channels]
    mid = product[channels : 2 * channels]
    high = product[2 * channels :]
    return shifted(low, 1) + mid + shifted(high, -1)


def clear_rims(field):
    depth, channels, lanes = field.shape
    rim = jnp.zeros((depth, channels, LANES), BF)
    field[:, :, :LANES] = rim
    field[:, :, lanes - LANES :] = rim


def arrive(refs, sems, target, up=1, width=1024):
    parts = len(refs) // 4 - 1
    copies = []
    for k in range(4):
        *bodies, rim = refs[k * (parts + 1) : (k + 1) * (parts + 1)]
        lanes = pl.ds(0, width)
        planes = 4 // parts
        pieces = [(body.at[:, :, lanes], up + n * planes, planes) for n, body in enumerate(bodies)]
        pieces.append((rim.at[pl.ds(0, up), :, lanes], 0, up))
        pieces.append((rim.at[pl.ds(rim.shape[0] - 1, 1), :, lanes], up + 4, 1))
        for n, (source, first, count) in enumerate(pieces):
            copies.append(pltpu.make_async_copy(source, target(k, first, count), sems.at[4 * k + n]))
    for copy in copies:
        copy.start()
    return copies


def assemble(field, me, refs, sems, channels, up=1, rim=1):
    def target(k, first, count):
        at = pl.multiple_of((me ^ k) * channels, channels)
        return field.at[pl.ds(first, count), pl.ds(at, channels), pl.ds(rim * LANES, 8 * LANES)]

    return arrive(refs, sems, target, up)


def turn_kernel(me_ref, filters, weights, kernel, sems):
    arrived = begin(filters.at[:, :, pl.ds(32, 16), pl.ds(0, LANES)], kernel, sems.at[0])
    arrived.wait()
    weights[...] = turned(me_ref[0], kernel, 32)


def third_kernel(me_ref, *refs):
    blocks, weights = refs[:8], refs[8]
    act, first, last, slope_out, own_out, front_out, row_out = refs[9:16]
    field, slope, front, row, sems = refs[16:]
    me = me_ref[0]

    def target(k, first, count):
        at = pl.multiple_of(LANES + (me ^ k) * (2 * LANES), LANES)
        return field.at[pl.ds(first, count), :, pl.ds(at, 2 * LANES)]

    copies = arrive(blocks, sems, target, 1, 2 * LANES)
    plane = begin(blocks[1].at[1], front.at[:, pl.ds(LANES, 256)], sems.at[21])

    @pl.when(me == 0)
    def _():
        front[:, :LANES] = jnp.zeros((64, LANES), BF)
        row[...] = jnp.zeros((4, 64, LANES), BF)

    for k in (1, 3):

        @pl.when((me > 0) & (me ^ k == me - 1))
        def _(k=k):
            begin(blocks[2 * k + 1].at[1, :, pl.ds(LANES, LANES)], front.at[:, pl.ds(0, LANES)], sems.at[22])
            begin(blocks[2 * k].at[:, :, pl.ds(256, LANES)], row, sems.at[23])

    clear_rims(field)
    plane.wait()

    @pl.when(me > 0)
    def _():
        corner = blocks[1].at[1, :, pl.ds(LANES, LANES)]
        pltpu.make_async_copy(corner, front.at[:, pl.ds(0, LANES)], sems.at[22]).wait()
        pltpu.make_async_copy(blocks[0].at[:, :, pl.ds(256, LANES)], row, sems.at[23]).wait()

    leaving = [begin(front, front_out, sems.at[24]), begin(row, row_out, sems.at[25])]
    for copy in copies:
        copy.wait()
    own = field.at[:, pl.ds(pl.multiple_of(me * 16, 16), 16), :]
    leaving.append(begin(own, own_out, sems.at[26]))
    for d in range(4):
        product = mm(weights[...], taps_of(field, d, 0, 1024))
        value, steep = activate(shift_sum(product, 32))
        act[d] = value.astype(BF)
        slope[d] = steep
    first[0] = act[0]
    last[0] = act[3]
    leaving.append(begin(slope, slope_out, sems.at[27]))
    for copy in leaving:
        copy.wait()


def fourth_kernel(me_ref, *refs):
    blocks, filters, cotangent = refs[:8], refs[8], refs[9]
    features, back, first, last, field, sems = refs[10:]
    me = me_ref[0]
    copies = assemble(field, me, blocks, sems, 32)
    clear_rims(field)
    weights = turned(me, filters.at[:, :, :32], 64)
    for copy in copies:
        copy.wait()
    for d in range(4):
        product = mm(weights, taps_of(field, d, 0, 1024))
        value, steep = activate(shift_sum(product, 64))
        features[d] = value.astype(BF)
        back[d] = (cotangent[d].astype(F32) * steep).astype(BF)
    first[0] = back[0]
    last[0] = back[3]


def flipped_weights(kernel):
    columns = []
    for a in range(3):
        for b in range(3):
            taps = [((2 - a) * 3 + 2 - b) * 3 + 2 - c for c in range(3)]
            columns.append(jnp.concatenate([kernel[t] for t in taps], 0))
    return jnp.concatenate(columns, 1)


def into_three_kernel(me_ref, *refs):
    blocks, kernel, slope = refs[:8], refs[8], refs[9]
    back, first, last, field, sems = refs[10:]
    copies = assemble(field, me_ref[0], blocks, sems, 64)
    clear_rims(field)
    weights = flipped_weights(kernel)
    for copy in copies:
        copy.wait()
    for d in range(4):
        product = mm(weights, taps_of(field, d, 0, 1024))
        back[d] = (shift_sum(product, 32) * slope[d]).astype(BF)
    first[0] = back[0]
    last[...] = back[2:]


def three_shifts(value):
    wide = value.astype(F32)
    return jnp.concatenate([shifted(wide, 1).astype(BF), value, shifted(wide, -1).astype(BF)], 0)


def filter_grad(wide, gradients):
    total = None
    for d in range(4):
        term = mm_nt(taps_of(wide, d, 0, 1024), gradients(d))
        total = term if total is None else total + term
    return total


def grad_four_kernel(me_ref, own, rim, *refs):
    blocks, grad, wide, gradient, sems = refs[:4], *refs[4:]
    copies = []
    for k in range(4):
        at = pl.multiple_of((me_ref[0] ^ k) * 64, 64)
        copies.append(begin(blocks[k], gradient.at[:, pl.ds(at, 64), :], sems.at[k]))
    clear_rims(wide)
    inside = slice(LANES, 9 * LANES)
    wide[0, :, inside] = three_shifts(rim[0])
    for d in range(4):
        wide[d + 1, :, inside] = three_shifts(own[d])
    wide[5, :, inside] = three_shifts(rim[1])
    for copy in copies:
        copy.wait()
    grad[...] = filter_grad(wide, lambda d: gradient[d]).astype(BF)


def last_kernel(me_ref, *refs):
    blocks = refs[:8]
    filters, w_back, act_two, grad_four = refs[8:12]
    slope, front, row, act_one, slope_one, volume = refs[12:18]
    out, field, shifts, wide, back_one, sems = refs[18:]
    me = me_ref[0]
    copies = assemble(field, me, blocks, sems, 32, up=2, rim=2)
    field[:, :, : 2 * LANES] = jnp.zeros((7, 128, 2 * LANES), BF)
    field[:, :, 10 * LANES :] = jnp.zeros((7, 128, LANES), BF)
    clear_rims(shifts)
    inside = slice(LANES, 9 * LANES)
    for d in range(6):
        shifts[d, :, inside] = three_shifts(act_two[d, :, inside])
    for t in range(27):
        out[t, :32] = grad_four[t]
    for t in range(27, 32):
        out[t] = jnp.zeros((48, 256), BF)
    taps = [jnp.concatenate([filters[j, t, 32:, :LANES] for j in range(4)], 0) for t in range(27)]
    weights = flipped_weights(taps)
    for copy in copies:
        copy.wait()

    start = pl.multiple_of(me * (2 * LANES), LANES)
    for d in range(5):
        steep = front[...].astype(F32)
        if d > 0:
            steep = jnp.concatenate([row[d - 1].astype(F32), slope[d - 1]], 1)
        product = mm(weights, taps_of(field, d, start, 3 * LANES))
        value = shift_sum(product, 64) * steep
        value = value.astype(BF)
        beside = shifted(value.astype(F32), 1).astype(BF)
        for h in range(3):
            wide[d, h, :64] = value[:, h * 128 : h * 128 + 128]
            wide[d, h, 64:] = beside[:, h * 128 : h * 128 + 128]
    for d_odd in range(2):
        for h_odd in range(2):
            taps = [(a, b) for a in ((1,) if d_odd else (0, 2)) for b in ((1,) if h_odd else (0, 2))]
            mixed = jnp.concatenate([w_back[a * 3 + b] for a, b in taps], 1)
            columns = []
            for d in range(4):
                for h in range(2):
                    parts = [wide[d + 1 - a // 2, h + 1 - b // 2] for a, b in taps]
                    columns.append(jnp.concatenate(parts, 0))
            into = mm(mixed, jnp.concatenate(columns, 1))
            for d in range(4):
                for h in range(2):
                    at = (d * 2 + h) * 128
                    lanes = slice((2 * h + h_odd) * 128, (2 * h + h_odd) * 128 + 128)
                    d_one = 2 * d + d_odd
                    value = into[:, at : at + 128] * slope_one[d_one, :, lanes]
                    back_one[d_one, :, lanes] = value.astype(BF)
    three = filter_grad(shifts, lambda d: field[d + 2, :, 2 * LANES : 10 * LANES]).astype(BF)
    for t in range(27):
        out[t, 32:, :128] = three[t * 16 : t * 16 + 16]
    two = None
    for d in range(4):
        columns = []
        for h in range(2):
            parts = [act_one[2 * d + a, h * 192 : h * 192 + 288] for a in range(3)]
            columns.append(jnp.concatenate(parts, 0))
        own = jnp.concatenate([wide[d + 1, 1, :64], wide[d + 1, 2, :64]], 1)
        term = mm_nt(jnp.concatenate(columns, 1), own)
        two = term if two is None else two + term
    one = None
    for d in range(8):
        columns = []
        for h in range(4):
            parts = [volume[2 * d + a, h * 64 : h * 64 + 96] for a in range(3)]
            columns.append(jnp.concatenate(parts, 0))
        term = mm_nt(jnp.concatenate(columns, 1), back_one[d])
        one = term if one is None else one + term
    both = jnp.concatenate([two, one], 0)
    for t in range(32):
        pair = [both[32 * t + 16 * q : 32 * t + 16 * q + 16] for q in range(2)]
        out[t, 32:, 128:] = jnp.concatenate(pair, 1).astype(BF)
    rest = [both[1024 + 32 * q : 1056 + 32 * q] for q in range(4)]
    out[27, :32] = jnp.concatenate(rest, 1).astype(BF)


def unpack_kernel(packed, grad_one, grad_two, grad_three, grad_four, both, sems):
    for t in range(27):
        grad_four[t] = packed[t, :32].astype(F32)
        grad_three[t] = packed[t, 32:, :128].astype(F32)
    for t in range(32):
        pair = packed[t, 32:, 128:].astype(F32)
        both[32 * t : 32 * t + 16] = pair[:, :64]
        both[32 * t + 16 : 32 * t + 32] = pair[:, 64:]
    rest = packed[27, :32].astype(F32)
    for q in range(4):
        both[1024 + 32 * q : 1056 + 32 * q] = rest[:, 64 * q : 64 * q + 64]
    grad_two[...] = both[:864]
    for t in range(9):
        at = 864 + 32 * t
        value = both[at : at + 12, :32] + both[at + 8 : at + 20, 32:]
        for c in range(3):
            grad_one[t // 3, t % 3, c] = value[4 * c : 4 * c + 4]


def moved(block, depth_step, chan_of):
    depth, chans = lax.axis_size("space"), lax.axis_size("chan")
    route = []
    for s in range(depth):
        for c in range(chans):
            to = chan_of(c)
            if 0 <= s + depth_step < depth and 0 <= to < chans:
                route.append((s * chans + c, (s + depth_step) * chans + to))
    return lax.ppermute(block, BOTH, route)


def gathered(own, first, last, meanwhile=None):
    across = [moved(part, 0, lambda c: c ^ 2) for part in own]
    up = moved(last, 1, lambda c: c)
    down = moved(first, -1, lambda c: c)
    core = [moved(part, 0, lambda c: c ^ 1) for part in own]
    rim = jnp.concatenate([up, down], 0)
    across_rim = moved(rim, 0, lambda c: c ^ 2)
    across, held, meanwhile = lax.optimization_barrier((across, rim, meanwhile))
    core_rim = moved(held, 0, lambda c: c ^ 1)
    pair = [moved(piece, 0, lambda c: c ^ 1) for piece in (*across, across_rim)]
    blocks = [*own, rim, *core, core_rim, *across, across_rim, *pair]
    return blocks if meanwhile is None else (blocks, meanwhile)


def summed(parts):
    terms = lax.all_to_all(parts, "space", 0, 0)
    own = jnp.sum(terms.astype(F32), 0)
    shape = own.shape
    row = lax.broadcasted_iota(jnp.int32, shape, 0)
    shared = (row >= 32) & (lane_of(shape) >= 128) | (lax.axis_index("space") == 27)
    both = own
    for step in (1, 2):
        sent = lax.optimization_barrier(both.astype(BF))
        both = sent.astype(F32) + moved(sent, 0, lambda c, step=step: c ^ step).astype(F32)
    total = jnp.where(shared, both, own).astype(BF)
    return lax.all_to_all(jnp.broadcast_to(total[None], parts.shape), "space", 0, 0)


def per_device(volume, kernel_one, kernel_two, kernel_three, kernel_four, cotangent):
    me = lax.axis_index("chan").astype(jnp.int32)[None]
    below = moved(volume[:, :3], -1, lambda c: c)
    beside = moved(volume[:, :, :3], 0, lambda c: c - 1)
    corner = moved(volume[:, :3, :3], -1, lambda c: c - 1)

    three = jnp.pad(kernel_three.reshape(27, 16, 128), ((0, 0), (0, 0), (0, 128)))
    four = kernel_four.reshape(27, 32, 256)
    filters = lax.all_gather(jnp.concatenate([four, three], 1), "chan")
    cotangent = jnp.transpose(cotangent.reshape(64, 4, 1024), (1, 0, 2))
    corner, cotangent = lax.optimization_barrier((corner, cotangent))

    even = jnp.pad(kernel_one, ((0, 0), (0, 0), (0, 5), (0, 0), (0, 0)))
    odd = jnp.pad(kernel_one, ((0, 0), (0, 0), (2, 3), (0, 0), (0, 0)))
    w_one = jnp.stack([even, odd]).reshape(2, 288, 32).transpose(0, 2, 1).reshape(64, 288)
    w_two = kernel_two.reshape(864, 64).T
    top = jnp.concatenate([kernel_two[:, :, 0], kernel_two[:, :, 2]], 3)
    bottom = jnp.pad(kernel_two[:, :, 1], ((0, 0), (0, 0), (0, 0), (0, 64)))
    w_back = jnp.concatenate([top, bottom], 2).reshape(9, 64, 128)

    tall = jnp.concatenate([volume, below], 1)
    side = jnp.pad(jnp.concatenate([beside, corner], 1), ((0, 0), (0, 0), (0, 5), (0, 0)))
    tall = jnp.concatenate([tall, side], 2)

    field, act_one, slope_one, body, first, last, slope_two = call(
        first_layers_kernel,
        [
            ((19, 352, 128), BF),
            ((9, 480, 128), BF),
            ((8, 64, 512), F32),
            ((4, 64, 384), BF),
            ((1, 64, 256), BF),
            ((2, 64, 256), BF),
            ((4, 64, 256), F32),
        ],
        [tall, w_one, w_two],
        [((19, 352, 128), BF), ((9, 480, 128), BF), ((8, 64, 512), F32)],
        away=(0, 1, 2),
    )
    pieces = range(1, 9)
    (w_three,) = call(
        turn_kernel, [((96, 576), BF)], [me, filters], [((4, 27, 16, 128), BF)], anywhere=(1,), far=(1,)
    )
    blocks, w_three = gathered([body], first, last, w_three)
    act_three, first, last, slope_three, own_two, front, row = call(
        third_kernel,
        [((4, 32, 1024), BF), ((1, 32, 1024), BF), ((1, 32, 1024), BF), ((4, 32, 1024), F32), ((6, 16, 1280), BF), ((64, 384), BF), ((4, 64, 128), BF)],
        [me, *blocks, w_three],
        [((6, 64, 1280), BF), ((4, 32, 1024), F32), ((64, 384), BF), ((4, 64, 128), BF)],
        anywhere=pieces,
        away=(3, 4, 5, 6),
    )
    blocks = gathered([act_three], first, last)
    features, back_four, first, last = call(
        fourth_kernel,
        [((4, 64, 1024), BF), ((4, 64, 1024), BF), ((1, 64, 1024), BF), ((1, 64, 1024), BF)],
        [me, *blocks, filters, cotangent],
        [((6, 128, 1280), BF)],
        anywhere=pieces,
    )
    features = jnp.transpose(features, (1, 0, 2)).reshape(64, 4, 8, 128)
    all_four = gathered([back_four], first, last)
    back_three, first, last = call(
        into_three_kernel,
        [((4, 32, 1024), BF), ((1, 32, 1024), BF), ((2, 32, 1024), BF)],
        [me, *all_four, four, slope_three],
        [((6, 256, 1280), BF)],
        anywhere=pieces,
    )
    (grad_four,) = call(
        grad_four_kernel,
        [((864, 256), BF)],
        [me, *blocks[:2], *all_four[::2]],
        [((6, 96, 1280), BF), ((4, 256, 1024), BF)],
        flops=2 * 864 * 256 * 4096,
        anywhere=range(3, 7),
    )
    blocks, grad_four = gathered([back_three], first, last, grad_four)
    (grads,) = call(
        last_kernel,
        [((32, 48, 256), BF)],
        [
            me,
            *blocks,
            filters,
            w_back,
            own_two,
            grad_four.reshape(27, 32, 256),
            slope_two,
            front,
            row,
            act_one,
            slope_one,
            field,
        ],
        [
            ((7, 128, 1408), BF),
            ((6, 48, 1280), BF),
            ((5, 3, 128, 128), BF),
            ((8, 64, 512), BF),
        ],
        anywhere=pieces,
    )
    grad_one, grad_two, grad_three, grad_four = call(
        unpack_kernel,
        [((3, 3, 3, 4, 32), F32), ((864, 64), F32), ((27, 16, 128), F32), ((27, 32, 256), F32)],
        [summed(grads)],
        [((1152, 64), F32)],
    )
    grad_two = grad_two.reshape(3, 3, 3, 32, 64)
    grad_three = grad_three.reshape(3, 3, 3, 16, 128)
    grad_four = grad_four.reshape(3, 3, 3, 32, 256)
    return (features, grad_one, grad_two, grad_three, grad_four)


def solution(mesh):
    in_specs = (
        P(None, "space", "chan", None),
        P(),
        P(),
        P(None, None, None, "chan", None),
        P(None, None, None, "chan", None),
        P("chan", "space", None, None),
    )
    out_specs = (
        P("chan", "space", None, None),
        P(),
        P(),
        P(None, None, None, "chan", None),
        P(None, None, None, "chan", None),
    )
    return jax.shard_map(
        per_device, mesh=mesh, in_specs=in_specs, out_specs=out_specs, check_vma=False
    )
```
